128 devices in a mesh: seq: 32 (over z, x, core), dp: 4 (over y).
Axes of the slice: x: 4, y: 4, z: 4, core: 2. Of those that a mesh axis runs over, the one named last changes fastest.
Arguments:
- queries: bfloat16 [65536, 2048], P(('dp', 'seq')), parts along dimension 0, may hold values from -150 to 150
- keys_values: bfloat16 [65536, 2, 2048], P(('dp', 'seq')), parts along dimension 0, may hold values from -4.5 to 4.5
- image_tiles: int32 [64], P('dp'), parts along dimension 0, may hold values from 1 to 8, 32 in all
- loader_tiles: int32 [128], P('dp'), parts along dimension 0, may hold values from 0 to 31, each once
Outputs:
- attended: bfloat16 [65536, 2048], P(('dp', 'seq')), parts along dimension 0
The draws below stay inside these ranges and needn't reach their ends.
There are 4 independent parts, one for each index of `dp`. The reference program is written for one: setup_inputs(seed, part) draws one part's arguments, and reference() takes and returns one part's arrays. A program takes and returns all parts, laid end to end along the dimension named above; each array names one. Nothing has to cross between parts.
Inputs may be any that keep to these rules, and one draw needn't show every extreme that they name: `image_tiles`: image sizes in tiles sum to 32; the largest is exactly 8. `loader_tiles`: each tile number appears once.
All inputs are finite; a program needn't handle non-finite values.
Results may differ from the reference program's by a relative error of at most 0.006.
Values may be sent and summed in bfloat16 or wider, within the bound.
A program may use at most 128 MiB of HBM per device.

```python
import math
import jax
import jax.numpy as jnp
import numpy as np
from jax import lax

H = 16
HD = 128
TILE = 512
NT = 32
TOKENS = 16384
MAXT = 8
IMGS = 16


def base_keys(key):
    return jnp.clip(jax.random.normal(key, (TOKENS, H * HD), jnp.float32), -4.0, 4.0)


def draw_keys_values(key, part):
    key_plane = base_keys(key)
    key = jax.random.fold_in(key, 11)
    value_plane = jnp.clip(jax.random.normal(key, (TOKENS, H * HD), jnp.float32), -4.0, 4.0)
    return jnp.stack([key_plane, value_plane], axis=1).astype(jnp.bfloat16)


def draw_queries(key, part):
    key = jax.random.fold_in(key, 7)
    return jnp.clip(jax.random.normal(key, (TOKENS, H * HD), jnp.float32), -4.0, 4.0).astype(jnp.bfloat16)


def length_profile(amount, total, reach, slope):
    weights = [(1 << 20) // math.isqrt(grade ** slope) + 1 for grade in range(2, amount + 1)]
    surplus, counts = total - reach - (amount - 1), [1] * (amount - 1)
    while surplus > 0:
        movable = [i for i in range(amount - 1) if counts[i] < reach]
        whole, left = sum([weights[i] for i in movable]), surplus
        for i in movable:
            addition = min(reach - counts[i], max(1, left * weights[i] // whole), surplus)
            counts[i] = counts[i] + addition
            surplus = surplus - addition
    return np.array([reach] + counts)


def uneven_parts(stream_key, count, total, most, lean):
    if count == 2:
        one = jax.random.randint(stream_key, (), max(1, total - most), min(most, total - 1) + 1)
        return jnp.stack([one, total - one])
    lengths = jnp.asarray(length_profile(count, total, most, lean), jnp.int32)
    pairs = (count - 1) // 2
    source_of, taker = lengths[1:1 + 2 * pairs:2], lengths[2:2 + 2 * pairs:2]
    margin = jnp.minimum(source_of - 1, most - taker)
    moved = jax.random.randint(jax.random.fold_in(stream_key, 1), (pairs,), 0, 1 << 20) % (margin + 1)
    lengths = lengths.at[1:1 + 2 * pairs:2].set(source_of - moved).at[2:2 + 2 * pairs:2].set(taker + moved)
    return lengths[jax.random.permutation(jax.random.fold_in(stream_key, 2), count)]


def setup_inputs(seed: int = 0, part: int = 0) -> dict:
    seeds = jax.random.split(jax.random.key(seed), 5)
    own_keys = jax.random.split(jax.random.fold_in(seeds[4], part), 5)
    return {
        "queries": draw_queries(jax.random.fold_in(jax.random.fold_in(seeds[4], part), 71), part),
        "keys_values": draw_keys_values(jax.random.fold_in(jax.random.fold_in(seeds[4], part), 71), part),
        "image_tiles": uneven_parts(own_keys[2], IMGS, NT, MAXT, 2).astype(jnp.int32),
        "loader_tiles": jax.random.permutation(own_keys[3], NT).astype(jnp.int32),
    }


def reference(queries, keys_values, image_tiles, loader_tiles):
    row_count = queries.shape[0]
    image_ends = jnp.cumsum(image_tiles).astype(jnp.int32)
    tile_ids = jnp.arange(NT, dtype=jnp.int32)
    tile_image = jnp.sum((image_ends[None, :] <= tile_ids[:, None]).astype(jnp.int32), axis=1).astype(jnp.int32)
    row_image = jnp.repeat(tile_image[loader_tiles], TILE).astype(jnp.int32)
    query_heads = queries.reshape(row_count, H, HD)
    key_heads = keys_values[:, 0].reshape(row_count, H, HD).astype(jnp.float32)
    value_heads = keys_values[:, 1].reshape(row_count, H, HD).astype(jnp.float32)
    score_scale = HD ** -0.5

    def one_block(block_index):
        start = (block_index * TILE).astype(jnp.int32)
        query_block = lax.dynamic_slice_in_dim(query_heads, start, TILE, 0).astype(jnp.float32)
        block_image = lax.dynamic_slice_in_dim(row_image, start, TILE, 0)
        allowed = block_image[:, None] == row_image[None, :]

        def one_head(head_index):
            query_one = lax.dynamic_index_in_dim(query_block, head_index, 1, keepdims=False)
            key_one = lax.dynamic_index_in_dim(key_heads, head_index, 1, keepdims=False)
            value_one = lax.dynamic_index_in_dim(value_heads, head_index, 1, keepdims=False)
            scores = jnp.einsum('qd,kd->qk', query_one, key_one) * score_scale
            scores = jnp.where(allowed, scores, -1e30)
            row_peak = jnp.max(scores, axis=1, keepdims=True)
            weights = jnp.where(allowed, jnp.exp(scores - row_peak), 0.0)
            denominator = jnp.sum(weights, axis=1, keepdims=True)
            rounded = lax.optimization_barrier(weights.astype(jnp.bfloat16))
            numerator = jnp.einsum('qk,kd->qd', rounded.astype(jnp.float32), value_one)
            return (numerator / denominator).astype(jnp.bfloat16)

        per_head = lax.map(one_head, jnp.arange(H, dtype=jnp.int32))
        return jnp.transpose(per_head, (1, 0, 2))

    blocks = lax.map(one_block, jnp.arange(NT, dtype=jnp.int32))
    return blocks.reshape(row_count, H * HD)
```

```python
import functools

import jax
import jax.numpy as jnp
from jax import lax
from jax.experimental import pallas as pl
from jax.experimental.pallas import tpu as pltpu
from jax.sharding import PartitionSpec as P

MESH = pl.DeviceIdType.MESH
HD = 128
HALF = 256
SIDE = 4
CHIPS = 16
DEVS = 32
MAXT = 8
STEPS = 150
UNROLL = 6
LISTS = 160
SCALE = HD**-0.5 * 1.4426950408889634
LOW = -1e30


def offset(n, core):
    m = ((15 - n) * 7) % CHIPS
    a, b = m // SIDE, m % SIDE
    return jnp.where(core == 0, a, b), jnp.where(core == 0, b, a)


def chip_at(chip, n, core, sign=1):
    dz, dx = offset(n, core)
    z, x = chip // SIDE, chip % SIDE
    return ((z + SIDE + sign * dz) % SIDE) * SIDE + (x + SIDE + sign * dx) % SIDE


def target(me, jj):
    core, chip = me % 2, me // 2
    n, e = jj // 2, jj % 2
    return chip_at(chip, n, core) * 2 + (core + 1 - e) % 2


def list_kernel(tiles_ref, loader_ref, qi_ref, kj_ref, first_ref, la_ref, last_ref, holder, begin, end):
    me = lax.axis_index("seq")

    def place(p, _):
        holder[loader_ref[p]] = p
        return 0

    lax.fori_loop(0, DEVS, place, 0)

    def image(m, start):
        stop = start + tiles_ref[m]

        def mark(t, _):
            begin[t] = start
            end[t] = stop
            return 0

        lax.fori_loop(start, stop, mark, 0)
        return stop

    lax.fori_loop(0, tiles_ref.shape[0], image, jnp.int32(0))

    def query(jj, s):
        p = target(me, jj)
        t = loader_ref[p]
        lo, hi = begin[t], end[t]
        stop = s + hi - lo

        def pair(t2, s):
            qi_ref[s] = p
            kj_ref[s] = holder[t2]
            first_ref[s] = (t2 == lo).astype(jnp.int32)
            la_ref[s] = stop - 1
            return s + 1

        s = lax.fori_loop(lo, hi, pair, s)
        last_ref[jj] = s - 1
        return s

    done = lax.fori_loop(0, DEVS, query, jnp.int32(0))

    def rest(s, _):
        qi_ref[s] = 0
        kj_ref[s] = 0
        first_ref[s] = 1
        la_ref[s] = 0
        return 0

    lax.fori_loop(done, LISTS, rest, 0)


def make_lists(image_tiles, loader_tiles):
    smem = pl.BlockSpec(memory_space=pltpu.SMEM)
    return pl.pallas_call(
        list_kernel,
        out_shape=[jax.ShapeDtypeStruct((LISTS,), jnp.int32)] * 4 + [jax.ShapeDtypeStruct((DEVS,), jnp.int32)],
        in_specs=[smem] * 2,
        out_specs=[smem] * 5,
        scratch_shapes=[pltpu.SMEM((DEVS,), jnp.int32)] * 3,
        name="lists",
    )(image_tiles, loader_tiles)


def dot_nt(a, b):
    return lax.dot_general(a, b, (((1,), (1,)), ((), ())), preferred_element_type=jnp.float32)


def dot_nn(a, b):
    return lax.dot_general(a, b, (((1,), (0,)), ((), ())), preferred_element_type=jnp.float32)


def attend_kernel(
    q_hbm,
    kv_hbm,
    qi,
    kj,
    first,
    la,
    last,
    out_hbm,
    pair,
    wide,
    stage,
    kv_a,
    kv_b,
    q,
    scores,
    probs,
    alpha,
    total,
    peak,
    slot_a,
    m_a,
    l_a,
    acc,
    slot_b,
    o_send,
    s_pair,
    s_q,
    r_q,
    s_kv,
    r_kv,
    s_fwd,
    s_o,
    r_o,
    s_own,
):
    me = lax.axis_index("seq")
    core, chip = me % 2, me // 2
    partner = chip * 2 + 1 - core
    kv = (kv_a, kv_b)

    def remote(src, dst, send, recv, device):
        return pltpu.make_async_remote_copy(
            src_ref=src, dst_ref=dst, send_sem=send, recv_sem=recv, device_id={"seq": device}, device_id_type=MESH
        )

    def cols(head):
        return pl.ds(pl.multiple_of(head * HD, HD), HD)

    def pair_load(head):
        return pltpu.make_async_copy(kv_hbm.at[:, :, cols(head)], pair.at[head], s_pair.at[head])

    def pair_loads(n, _):
        pair_load(chip_at(chip, n, core)).start()
        return 0

    lax.fori_loop(0, CHIPS, pair_loads, 0)

    barrier = pltpu.get_barrier_semaphore()
    for d in range(1, DEVS):
        pl.semaphore_signal(barrier, inc=1, device_id={"seq": (me + d) % DEVS}, device_id_type=MESH)
    pl.semaphore_wait(barrier, DEVS - 1)

    def q_copy(jj):
        device = target(me, jj)
        rows = pl.ds(pl.multiple_of((device % 2) * HALF, HALF), HALF)
        return remote(q_hbm.at[rows, cols(device // 2)], q.at[me], s_q.at[jj], r_q.at[me], device)

    def q_sends(jj, _):
        q_copy(jj).start()
        return 0

    lax.fori_loop(0, DEVS - 1, q_sends, 0)
    own_rows = pl.ds(pl.multiple_of(core * HALF, HALF), HALF)
    own_q = pltpu.make_async_copy(q_hbm.at[own_rows, cols(chip)], q.at[me], s_own.at[0])
    own_q.start()

    def kv_copy(u, n):
        t = chip_at(chip, n, core)
        return remote(stage.at[t, u], kv[u].at[me], s_kv.at[u, n], r_kv.at[u, me], t * 2 + core)

    def split(n, _):
        t = chip_at(chip, n, core)
        pair_load(t).wait()
        wide[...] = pair[t].reshape(2 * 2 * HALF, HD).astype(jnp.float32)
        keys = wide[pl.ds(0, 2 * HALF, stride=2), :].astype(jnp.bfloat16)
        values = wide[pl.ds(1, 2 * HALF, stride=2), :].T.astype(jnp.bfloat16)
        for u in range(2):
            stage[t, u, 0:HALF] = keys[u * HALF : (u + 1) * HALF]
            stage[t, u, HALF : HALF + HD] = values[:, u * HALF : u * HALF + HD]
            stage[t, u, HALF + HD : 2 * HALF] = values[:, u * HALF + HD : (u + 1) * HALF]

        @pl.when(n < CHIPS - 1)
        def _():
            kv_copy(0, n).start()

        return 0

    lax.fori_loop(0, CHIPS, split, 0)

    def kv_sends(n, _):
        kv_copy(1, n).start()
        return 0

    lax.fori_loop(0, CHIPS - 1, kv_sends, 0)
    own_kv = [pltpu.make_async_copy(stage.at[chip, u], kv[u].at[me], s_own.at[1 + u]) for u in range(2)]
    own_fwd = [
        remote(stage.at[chip, u], kv[u].at[me], s_fwd.at[u, CHIPS - 1], r_kv.at[u, me], partner) for u in range(2)
    ]
    for u in range(2):
        own_kv[u].start()
        own_fwd[u].start()

    def forward_copy(u, n):
        p = chip_at(chip, n, core, -1) * 2 + core
        return remote(kv[u].at[p], kv[u].at[p], s_fwd.at[u, n], r_kv.at[u, p], partner)

    def forward(u):
        def step(n, _):
            copy = forward_copy(u, n)
            copy.wait_recv()
            copy.start()
            return 0

        return step

    def kv_arrive(u):
        def step(c, _):
            p = c * 2 + 1 - core
            remote(kv[u].at[p], kv[u].at[p], s_fwd.at[u, 0], r_kv.at[u, p], partner).wait_recv()
            return 0

        lax.fori_loop(0, CHIPS, step, 0)

    lax.fori_loop(0, CHIPS - 1, forward(0), 0)

    def q_arrive(d, _):
        p = (me + d) % DEVS
        remote(q.at[p], q.at[p], s_q.at[0], r_q.at[p], partner).wait_recv()
        return 0

    lax.fori_loop(1, DEVS, q_arrive, 0)
    own_q.wait()
    own_kv[0].wait()
    kv_arrive(0)

    def stage_scores(u, s, w):
        sc = dot_nt(kv[u][kj[s], 0:HALF], q[qi[s]])
        scores[w] = sc
        peak[w] = jnp.max(sc, axis=0, keepdims=True) * SCALE

    def stage_weights(u, s, w, carry):
        m, l = carry
        new = first[s] == 1
        m = jnp.where(new, LOW if u == 0 else m_a[la[s]], m)
        l = jnp.where(new, 0.0 if u == 0 else l_a[la[s]], l)
        m_new = jnp.maximum(m, peak[w])
        p = jnp.exp2(scores[w] * SCALE - m_new)
        al = jnp.exp2(m - m_new)
        l = l * al + jnp.sum(p, axis=0, keepdims=True)
        probs[w] = p.astype(jnp.bfloat16)
        alpha[w] = al
        if u == 0:
            m_a[s] = m_new
            l_a[s] = l
        else:
            total[w] = l
        return m_new, l

    def stage_values(u, s, w):
        j = kj[s]
        d = dot_nn(kv[u][j, HALF : HALF + HD], probs[w, 0:HD]) + dot_nn(
            kv[u][j, HALF + HD : 2 * HALF], probs[w, HD : 2 * HD]
        )
        prev = acc[...]
        if u == 1:
            prev = jnp.where(first[s] == 1, slot_a[la[s]], prev)
        a = prev * alpha[w] + d
        acc[...] = a
        if u == 0:
            slot_a[s] = a
        else:
            slot_b[s] = (a * (1.0 / total[w])).astype(jnp.bfloat16)

    def attend(u, beside):
        ahead_s, ahead_w = 4, 2
        acc[...] = jnp.zeros_like(acc)
        carry = (jnp.zeros((1, HALF), jnp.float32), jnp.zeros((1, HALF), jnp.float32))
        for s in range(ahead_s):
            stage_scores(u, s, s)
        for s in range(ahead_w):
            carry = stage_weights(u, s, s, carry)

        def body(t, carry):
            for w in range(UNROLL):
                s = t * UNROLL + w
                stage_values(u, s, w)
                stage_scores(u, s + ahead_s, (w + ahead_s) % UNROLL)
                carry = stage_weights(u, s + ahead_w, (w + ahead_w) % UNROLL, carry)
            beside(t)
            return carry

        lax.fori_loop(0, STEPS // UNROLL, body, carry)

    def forwards_due(t):
        return jnp.clip(t - 8, 0, CHIPS - 1)

    def beside_a(t):
        lax.fori_loop(forwards_due(t), forwards_due(t + 1), forward(1), 0)

    attend(0, beside_a)
    own_kv[1].wait()
    kv_arrive(1)

    def o_copy(jj):
        out_rows = pl.ds(pl.multiple_of(core * HALF, HALF), HALF)
        return remote(o_send.at[jj], out_hbm.at[out_rows, cols(chip)], s_o.at[jj], r_o.at[me], target(me, jj))

    own_o = pltpu.make_async_copy(o_send.at[DEVS - 1], out_hbm.at[own_rows, cols(chip)], s_own.at[3])

    def emit(jj, _):
        o_send[jj] = slot_b[last[jj]].astype(jnp.float32).T.astype(jnp.bfloat16)

        @pl.when(jj < DEVS - 1)
        def _():
            o_copy(jj).start()

        @pl.when(jj == DEVS - 1)
        def _():
            own_o.start()

        return 0

    def outputs_due(t):
        s = t * UNROLL
        return jnp.clip(jnp.maximum(s // MAXT, s - (STEPS - DEVS)), 0, DEVS)

    def beside_b(t):
        lax.fori_loop(outputs_due(t), outputs_due(t + 1), emit, 0)

    attend(1, beside_b)

    def q_sent(jj, _):
        q_copy(jj).wait_send()
        return 0

    lax.fori_loop(0, DEVS - 1, q_sent, 0)
    for u in range(2):

        def kv_sent(n, _, u=u):
            kv_copy(u, n).wait_send()
            forward_copy(u, n).wait_send()
            return 0

        lax.fori_loop(0, CHIPS - 1, kv_sent, 0)
        own_fwd[u].wait_send()

    def o_sent(jj, _):
        o_copy(jj).wait_send()
        return 0

    lax.fori_loop(0, DEVS - 1, o_sent, 0)
    own_o.wait()

    def o_arrive(d, _):
        p = (me + d) % DEVS
        rows = pl.ds(pl.multiple_of((p % 2) * HALF, HALF), HALF)
        remote(o_send.at[0], out_hbm.at[rows, cols(p // 2)], s_o.at[0], r_o.at[p], partner).wait_recv()
        return 0

    lax.fori_loop(1, DEVS, o_arrive, 0)


def local(queries, keys_values, image_tiles, loader_tiles):
    lists = make_lists(image_tiles, loader_tiles)
    bf16, f32 = jnp.bfloat16, jnp.float32
    anywhere = pl.BlockSpec(memory_space=pl.ANY)
    smem = pl.BlockSpec(memory_space=pltpu.SMEM)
    dma = pltpu.SemaphoreType.DMA
    return pl.pallas_call(
        attend_kernel,
        out_shape=jax.ShapeDtypeStruct(queries.shape, bf16),
        in_specs=[anywhere] * 2 + [smem] * 5,
        out_specs=anywhere,
        scratch_shapes=[
            pltpu.VMEM((CHIPS, 2 * HALF, 2, HD), bf16),
            pltpu.VMEM((4 * HALF, HD), f32),
            pltpu.VMEM((CHIPS, 2, 2 * HALF, HD), bf16),
            pltpu.VMEM((DEVS, 2 * HALF, HD), bf16),
            pltpu.VMEM((DEVS, 2 * HALF, HD), bf16),
            pltpu.VMEM((DEVS, HALF, HD), bf16),
            pltpu.VMEM((UNROLL, HALF, HALF), f32),
            pltpu.VMEM((UNROLL, HALF, HALF), bf16),
            pltpu.VMEM((UNROLL, 1, HALF), f32),
            pltpu.VMEM((UNROLL, 1, HALF), f32),
            pltpu.VMEM((UNROLL, 1, HALF), f32),
            pltpu.VMEM((STEPS, HD, HALF), f32),
            pltpu.VMEM((LISTS, 1, HALF), f32),
            pltpu.VMEM((LISTS, 1, HALF), f32),
            pltpu.VMEM((HD, HALF), f32),
            pltpu.VMEM((STEPS, HD, HALF), bf16),
            pltpu.VMEM((DEVS, HALF, HD), bf16),
            dma((CHIPS,)),
            dma((DEVS,)),
            dma((DEVS,)),
            dma((2, CHIPS)),
            dma((2, DEVS)),
            dma((2, CHIPS)),
            dma((DEVS,)),
            dma((DEVS,)),
            dma((4,)),
        ],
        compiler_params=pltpu.CompilerParams(collective_id=0, has_side_effects=True, vmem_limit_bytes=62 << 20),
        name="attend",
    )(queries, keys_values, *lists)


def solution(mesh):
    in_specs = (P(("dp", "seq"), None), P(("dp", "seq"), None, None), P("dp"), P("dp"))
    out_specs = P(("dp", "seq"), None)
    return jax.shard_map(local, mesh=mesh, in_specs=in_specs, out_specs=out_specs, check_vma=False)
```

```python
import functools

import jax
import jax.numpy as jnp
from jax import lax
from jax.experimental import pallas as pl
from jax.experimental.pallas import tpu as pltpu
from jax.sharding import PartitionSpec as P

MESH = pl.DeviceIdType.MESH
HD = 128
HALF = 256
SIDE = 4
CHIPS = 16
DEVS = 32
MAX_UNITS = 4
UNITS = 84
MOST = 83
UNROLL = 6
LISTS = 96
SCALE = HD**-0.5 * 1.4426950408889634
LOW = -1e30


def offset(n, core):
    m = ((15 - n) * 7) % CHIPS
    a, b = m // SIDE, m % SIDE
    return jnp.where(core == 0, a, b), jnp.where(core == 0, b, a)


def chip_at(chip, n, core, sign=1):
    dz, dx = offset(n, core)
    z, x = chip // SIDE, chip % SIDE
    return ((z + SIDE + sign * dz) % SIDE) * SIDE + (x + SIDE + sign * dx) % SIDE


def target(me, jj):
    core, chip = me % 2, me // 2
    n, e = jj // 2, jj % 2
    return chip_at(chip, n, core) * 2 + (core + 1 - e) % 2


def fill_lists(me, tiles, loader, order, holder, begin, end, last, lists):
    qi, k1, k2, pairs, first, la = lists
    images = tiles.shape[0]

    def place(t, _):
        order[t] = target(me, t)
        at = jnp.int32(0)
        for p in range(DEVS):
            at = at + jnp.where(loader[p] == t, p, 0)
        holder[t] = at
        return 0

    lax.fori_loop(0, DEVS, place, 0)

    def image(t, carry):
        m, start, stop = carry
        new = t == stop
        m = jnp.where(new, jnp.minimum(m + 1, images - 1), m)
        start = jnp.where(new, stop, start)
        stop = jnp.where(new, stop + tiles[m], stop)
        begin[t] = start
        end[t] = stop
        return m, start, stop

    lax.fori_loop(0, DEVS, image, (jnp.int32(0), jnp.int32(0), tiles[0]))

    def finish(jj, total):
        t = loader[order[jj]]
        size = end[t] - begin[t]
        total = total + 1
        for more in (2, 4, 6):
            total = total + jnp.where(size > more, 1, 0)
        last[jj] = jnp.minimum(total - 1, UNITS - 1)
        return total

    lax.fori_loop(0, DEVS, finish, jnp.int32(0))

    def unit(s, carry):
        jj, r = carry
        p = order[jj]
        t = loader[p]
        lo, hi = begin[t], end[t]
        one = jnp.minimum(lo + 2 * r, hi - 1)
        two = jnp.minimum(one + 1, hi - 1)
        qi[s] = p
        k1[s] = holder[one]
        k2[s] = holder[two]
        pairs[s] = two - one
        first[s] = (r == 0).astype(jnp.int32)
        la[s] = last[jj]
        more = 2 * r + 2 < hi - lo
        return jnp.where(more, jj, jnp.minimum(jj + 1, DEVS - 1)), jnp.where(more, r + 1, 0)

    lax.fori_loop(0, LISTS, unit, (jnp.int32(0), jnp.int32(0)))


def dot_nt(a, b):
    return lax.dot_general(a, b, (((1,), (1,)), ((), ())), preferred_element_type=jnp.float32)


def dot_nn(a, b):
    return lax.dot_general(a, b, (((1,), (0,)), ((), ())), preferred_element_type=jnp.float32)


def attend_kernel(
    q_hbm,
    kv_hbm,
    last,
    qi,
    k1,
    k2,
    pairs,
    first,
    la,
    out_hbm,
    pair,
    wide,
    stage,
    kv_a,
    kv_b,
    q,
    scores,
    probs,
    alpha,
    total,
    peak,
    slot_a,
    m_a,
    l_a,
    acc,
    slot_b,
    o_send,
    s_pair,
    s_q,
    r_q,
    s_kv,
    r_kv,
    s_fwd,
    s_o,
    r_o,
    s_own,
):
    me = lax.axis_index("seq")
    core, chip = me % 2, me // 2
    partner = chip * 2 + 1 - core
    kv = (kv_a, kv_b)

    def remote(src, dst, send, recv, device):
        return pltpu.make_async_remote_copy(
            src_ref=src, dst_ref=dst, send_sem=send, recv_sem=recv, device_id={"seq": device}, device_id_type=MESH
        )

    def cols(head):
        return pl.ds(pl.multiple_of(head * HD, HD), HD)

    def pair_load(head):
        return pltpu.make_async_copy(kv_hbm.at[:, :, cols(head)], pair.at[head], s_pair.at[head])

    def pair_loads(n, _):
        pair_load(chip_at(chip, n, core)).start()
        return 0

    lax.fori_loop(0, CHIPS, pair_loads, 0)

    barrier = pltpu.get_barrier_semaphore()
    for d in range(1, DEVS):
        pl.semaphore_signal(barrier, inc=1, device_id={"seq": (me + d) % DEVS}, device_id_type=MESH)
    pl.semaphore_wait(barrier, DEVS - 1)

    def q_copy(jj):
        device = target(me, jj)
        rows = pl.ds(pl.multiple_of((device % 2) * HALF, HALF), HALF)
        return remote(q_hbm.at[rows, cols(device // 2)], q.at[me], s_q.at[jj], r_q.at[me], device)

    def q_sends(jj, _):
        q_copy(jj).start()
        return 0

    lax.fori_loop(0, DEVS - 1, q_sends, 0)
    own_rows = pl.ds(pl.multiple_of(core * HALF, HALF), HALF)
    own_q = pltpu.make_async_copy(q_hbm.at[own_rows, cols(chip)], q.at[me], s_own.at[0])
    own_q.start()

    def kv_copy(u, n):
        t = chip_at(chip, n, core)
        return remote(stage.at[t, u], kv[u].at[me], s_kv.at[u, n], r_kv.at[u, me], t * 2 + core)

    def split(n, _):
        t = chip_at(chip, n, core)
        pair_load(t).wait()
        wide[...] = pair[t].reshape(2 * 2 * HALF, HD).astype(jnp.float32)
        keys = wide[pl.ds(0, 2 * HALF, stride=2), :].astype(jnp.bfloat16)
        values = wide[pl.ds(1, 2 * HALF, stride=2), :].T.astype(jnp.bfloat16)
        for u in range(2):
            stage[t, u, 0:HALF] = keys[u * HALF : (u + 1) * HALF]
            stage[t, u, HALF : HALF + HD] = values[:, u * HALF : u * HALF + HD]
            stage[t, u, HALF + HD : 2 * HALF] = values[:, u * HALF + HD : (u + 1) * HALF]

        @pl.when(n < CHIPS - 1)
        def _():
            kv_copy(0, n).start()

        return 0

    lax.fori_loop(0, CHIPS, split, 0)

    def kv_sends(n, _):
        kv_copy(1, n).start()
        return 0

    lax.fori_loop(0, CHIPS - 1, kv_sends, 0)
    own_kv = [pltpu.make_async_copy(stage.at[chip, u], kv[u].at[me], s_own.at[1 + u]) for u in range(2)]
    own_fwd = [
        remote(stage.at[chip, u], kv[u].at[me], s_fwd.at[u, CHIPS - 1], r_kv.at[u, me], partner) for u in range(2)
    ]
    for u in range(2):
        own_kv[u].start()
        own_fwd[u].start()

    def forward_copy(u, n):
        p = chip_at(chip, n, core, -1) * 2 + core
        return remote(kv[u].at[p], kv[u].at[p], s_fwd.at[u, n], r_kv.at[u, p], partner)

    def forward(u):
        def step(n, _):
            copy = forward_copy(u, n)
            copy.wait_recv()
            copy.start()
            return 0

        return step

    def kv_arrive(u):
        def step(c, _):
            p = c * 2 + 1 - core
            remote(kv[u].at[p], kv[u].at[p], s_fwd.at[u, 0], r_kv.at[u, p], partner).wait_recv()
            return 0

        lax.fori_loop(0, CHIPS, step, 0)

    def q_arrive(d, _):
        p = (me + d) % DEVS
        remote(q.at[p], q.at[p], s_q.at[0], r_q.at[p], partner).wait_recv()
        return 0

    lax.fori_loop(1, DEVS, q_arrive, 0)
    own_q.wait()

    lax.fori_loop(0, CHIPS - 1, forward(0), 0)
    own_kv[0].wait()
    kv_arrive(0)

    def stage_scores(u, s, w):
        keys = jnp.concatenate([kv[u][k1[s], 0:HALF], kv[u][k2[s], 0:HALF]], axis=0)
        sc = dot_nt(keys, q[qi[s]])
        scores[w] = sc
        one = jnp.max(sc[0:HALF], axis=0, keepdims=True)
        two = jnp.max(sc[HALF : 2 * HALF], axis=0, keepdims=True)
        peak[w] = jnp.where(pairs[s] == 1, jnp.maximum(one, two), one) * SCALE

    def stage_weights(u, s, w, carry):
        m, l = carry
        new = first[s] == 1
        m = jnp.where(new, LOW if u == 0 else m_a[la[s]], m)
        l = jnp.where(new, 0.0 if u == 0 else l_a[la[s]], l)
        m_new = jnp.maximum(m, peak[w])
        m_two = jnp.where(pairs[s] == 1, m_new, -LOW)
        al = jnp.exp2(m - m_new)
        l = l * al
        for x, m_x in enumerate((m_new, m_two)):
            rows = pl.ds(x * HALF, HALF)
            p = jnp.exp2(scores[w, rows] * SCALE - m_x)
            l = l + jnp.sum(p, axis=0, keepdims=True)
            probs[w, rows] = p.astype(jnp.bfloat16)
        alpha[w] = al
        if u == 0:
            m_a[s] = m_new
            l_a[s] = l
        else:
            total[w] = l
        return m_new, l

    def stage_values(u, s, w):
        blocks = [kv[u][k[s], HALF + x * HD : HALF + (x + 1) * HD] for k in (k1, k2) for x in range(2)]
        d = dot_nn(jnp.concatenate(blocks, axis=1), probs[w])
        prev = acc[...]
        if u == 1:
            prev = jnp.where(first[s] == 1, slot_a[la[s]], prev)
        a = prev * alpha[w] + d
        acc[...] = a
        if u == 0:
            slot_a[s] = a
        else:
            slot_b[s] = (a * (1.0 / total[w])).astype(jnp.bfloat16)

    def attend(u, beside):
        ahead_s, ahead_w = 4, 2
        acc[...] = jnp.zeros_like(acc)
        carry = (jnp.zeros((1, HALF), jnp.float32), jnp.zeros((1, HALF), jnp.float32))
        for s in range(ahead_s):
            stage_scores(u, s, s)
        for s in range(ahead_w):
            carry = stage_weights(u, s, s, carry)

        def body(t, carry):
            for w in range(UNROLL):
                s = t * UNROLL + w
                stage_values(u, s, w)
                stage_scores(u, s + ahead_s, (w + ahead_s) % UNROLL)
                carry = stage_weights(u, s + ahead_w, (w + ahead_w) % UNROLL, carry)
            beside(t)
            return carry

        lax.fori_loop(0, UNITS // UNROLL, body, carry)

    def forwards_due(t):
        return jnp.clip(t - 2, 0, CHIPS - 1)

    def beside_a(t):
        lax.fori_loop(forwards_due(t), forwards_due(t + 1), forward(1), 0)

    attend(0, beside_a)
    lax.fori_loop(UNITS // UNROLL - 2, CHIPS - 1, forward(1), 0)
    own_kv[1].wait()
    kv_arrive(1)

    def o_copy(jj):
        out_rows = pl.ds(pl.multiple_of(core * HALF, HALF), HALF)
        return remote(o_send.at[jj], out_hbm.at[out_rows, cols(chip)], s_o.at[jj], r_o.at[me], target(me, jj))

    own_o = pltpu.make_async_copy(o_send.at[DEVS - 1], out_hbm.at[own_rows, cols(chip)], s_own.at[3])

    def emit(jj, _):
        o_send[jj] = slot_b[last[jj]].astype(jnp.float32).T.astype(jnp.bfloat16)

        @pl.when(jj < DEVS - 1)
        def _():
            o_copy(jj).start()

        @pl.when(jj == DEVS - 1)
        def _():
            own_o.start()

        return 0

    def outputs_due(t):
        s = t * UNROLL
        return jnp.clip(jnp.maximum(s // MAX_UNITS, s - (MOST - DEVS)), 0, DEVS)

    def beside_b(t):
        lax.fori_loop(outputs_due(t), outputs_due(t + 1), emit, 0)

    attend(1, beside_b)

    def q_sent(jj, _):
        q_copy(jj).wait_send()
        return 0

    lax.fori_loop(0, DEVS - 1, q_sent, 0)
    for u in range(2):

        def kv_sent(n, _, u=u):
            kv_copy(u, n).wait_send()
            forward_copy(u, n).wait_send()
            return 0

        lax.fori_loop(0, CHIPS - 1, kv_sent, 0)
        own_fwd[u].wait_send()

    def o_sent(jj, _):
        o_copy(jj).wait_send()
        return 0

    lax.fori_loop(0, DEVS - 1, o_sent, 0)
    own_o.wait()

    def o_arrive(d, _):
        p = (me + d) % DEVS
        rows = pl.ds(pl.multiple_of((p % 2) * HALF, HALF), HALF)
        remote(o_send.at[0], out_hbm.at[rows, cols(p // 2)], s_o.at[0], r_o.at[p], partner).wait_recv()
        return 0

    lax.fori_loop(1, DEVS, o_arrive, 0)


def local(queries, keys_values, image_tiles, loader_tiles):
    bf16, f32 = jnp.bfloat16, jnp.float32
    anywhere = pl.BlockSpec(memory_space=pl.ANY)
    smem = pl.BlockSpec(memory_space=pltpu.SMEM)
    dma = pltpu.SemaphoreType.DMA

    def list_kernel(tiles, loader, last, qi, k1, k2, pairs, first, la, order, holder, begin, end):
        me = lax.axis_index("seq")
        fill_lists(me, tiles, loader, order, holder, begin, end, last, (qi, k1, k2, pairs, first, la))

    lists = pl.pallas_call(
        list_kernel,
        out_shape=[jax.ShapeDtypeStruct((DEVS,), jnp.int32)] + [jax.ShapeDtypeStruct((LISTS,), jnp.int32)] * 6,
        in_specs=[smem] * 2,
        out_specs=[smem] * 7,
        scratch_shapes=[pltpu.SMEM((DEVS,), jnp.int32)] * 4,
        name="lists",
    )(image_tiles, loader_tiles)
    return pl.pallas_call(
        attend_kernel,
        out_shape=jax.ShapeDtypeStruct(queries.shape, bf16),
        in_specs=[anywhere] * 2 + [smem] * 7,
        out_specs=anywhere,
        scratch_shapes=[
            pltpu.VMEM((CHIPS, 2 * HALF, 2, HD), bf16),
            pltpu.VMEM((4 * HALF, HD), f32),
            pltpu.VMEM((CHIPS, 2, 2 * HALF, HD), bf16),
            pltpu.VMEM((DEVS, 2 * HALF, HD), bf16),
            pltpu.VMEM((DEVS, 2 * HALF, HD), bf16),
            pltpu.VMEM((DEVS, HALF, HD), bf16),
            pltpu.VMEM((UNROLL, 2 * HALF, HALF), f32),
            pltpu.VMEM((UNROLL, 2 * HALF, HALF), bf16),
            pltpu.VMEM((UNROLL, 1, HALF), f32),
            pltpu.VMEM((UNROLL, 1, HALF), f32),
            pltpu.VMEM((UNROLL, 1, HALF), f32),
            pltpu.VMEM((UNITS, HD, HALF), f32),
            pltpu.VMEM((LISTS, 1, HALF), f32),
            pltpu.VMEM((LISTS, 1, HALF), f32),
            pltpu.VMEM((HD, HALF), f32),
            pltpu.VMEM((UNITS, HD, HALF), bf16),
            pltpu.VMEM((DEVS, HALF, HD), bf16),
            dma((CHIPS,)),
            dma((DEVS,)),
            dma((DEVS,)),
            dma((2, CHIPS)),
            dma((2, DEVS)),
            dma((2, CHIPS)),
            dma((DEVS,)),
            dma((DEVS,)),
            dma((4,)),
        ],
        compiler_params=pltpu.CompilerParams(collective_id=0, has_side_effects=True, vmem_limit_bytes=62 << 20),
        name="attend",
    )(queries, keys_values, *lists)


def solution(mesh):
    in_specs = (P(("dp", "seq"), None), P(("dp", "seq"), None, None), P("dp"), P("dp"))
    out_specs = P(("dp", "seq"), None)
    return jax.shard_map(local, mesh=mesh, in_specs=in_specs, out_specs=out_specs, check_vma=False)
```

```python
import functools

import jax
import jax.numpy as jnp
from jax import lax
from jax.experimental import pallas as pl
from jax.experimental.pallas import tpu as pltpu
from jax.sharding import PartitionSpec as P

MESH = pl.DeviceIdType.MESH
HD = 128
HALF = 256
SIDE = 4
CHIPS = 16
DEVS = 32
MAX_UNITS = 4
UNITS = 84
MOST = 83
UNROLL = 6
LISTS = 128
SCALE = HD**-0.5 * 1.4426950408889634
LOW = -1e30


ORDER = ((2, 0), (0, 2), (2, 1), (2, 3), (1, 2), (3, 2), (2, 2), (1, 0), (3, 0), (0, 1), (0, 3), (1, 1), (3, 3), (1, 3), (3, 1))


def offset(n, core):
    a, b = jnp.zeros_like(n), jnp.zeros_like(n)
    for k, (along_z, along_x) in enumerate(ORDER):
        a = jnp.where(n == k, along_z, a)
        b = jnp.where(n == k, along_x, b)
    return jnp.where(core == 0, a, b), jnp.where(core == 0, b, a)


def chip_at(chip, n, core, sign=1):
    dz, dx = offset(n, core)
    z, x = chip // SIDE, chip % SIDE
    return ((z + SIDE + sign * dz) % SIDE) * SIDE + (x + SIDE + sign * dx) % SIDE


def target(me, jj):
    core, chip = me % 2, me // 2
    n, e = jj // 2, jj % 2
    return chip_at(chip, n, core) * 2 + (core + 1 - e) % 2


def list_kernel(tiles_ref, loader_ref, lists_ref):
    me = lax.axis_index("seq")
    f32 = jnp.float32
    images = tiles_ref.shape[0]

    def grid(shape, axis):
        return lax.broadcasted_iota(jnp.int32, shape, axis)

    def pick(mask, values, axis):
        return jnp.sum(jnp.where(mask, values, 0.0), axis=axis, keepdims=True)

    def across(ref):
        n = ref.shape[0]
        values = jnp.zeros((1, n), jnp.int32)
        for i in range(n):
            values = jnp.where(grid((1, n), 1) == i, ref[i], values)
        return values.astype(f32)

    tiles, loader = across(tiles_ref), across(loader_ref)
    row, col = grid((DEVS, DEVS), 0), grid((DEVS, DEVS), 1)
    image_row, image_col = grid((images, images), 0), grid((images, images), 1)
    loader_down = pick(row == col, loader, 1)
    tiles_down = pick(image_row == image_col, tiles, 1)
    ends = pick(image_row <= image_col, tiles_down, 0)
    starts = ends - tiles
    place = target(me, grid((DEVS, 1), 0))
    tile = pick(place == col, loader, 1)
    lo, hi = pick(ends <= tile, tiles, 1), pick(starts <= tile, tiles, 1)
    count = jnp.floor((hi - lo + 1.0) * 0.5)
    after = pick(col <= row, pick(row == col, count, 0), 1)
    before = after - count
    s = grid((1, LISTS), 1).astype(f32)
    mine = (before <= s) & (s < after)
    r = s - pick(mine, before, 0)
    one = pick(mine, lo, 0) + 2.0 * r
    two = jnp.minimum(one + 1.0, pick(mine, hi, 0) - 1.0)
    down = grid((DEVS, LISTS), 0)
    devices = down.astype(f32)
    live = s < jnp.sum(count, axis=0, keepdims=True)
    lists = (
        pick(mine, place.astype(f32), 0),
        pick(loader_down == one, devices, 0),
        pick(loader_down == two, devices, 0),
        jnp.where(live, two - one, 0.0),
        jnp.where(live, jnp.where(r == 0.0, 1.0, 0.0), 1.0),
        pick(mine, after - 1.0, 0),
        pick(down == grid((DEVS, LISTS), 1), after - 1.0, 0),
    )
    for i, values in enumerate(lists):
        lists_ref[i : i + 1, :] = values.astype(jnp.int32)
    lists_ref[len(lists) : len(lists) + 1, :] = jnp.zeros((1, LISTS), jnp.int32)


def dot_nn(a, b):
    return lax.dot_general(a, b, (((1,), (0,)), ((), ())), preferred_element_type=jnp.float32)


def attend_kernel(
    q_hbm,
    kv_hbm,
    lists,
    out_hbm,
    pair,
    wide,
    stage,
    kv_a,
    kv_b,
    q,
    q_t,
    scores,
    probs,
    alpha,
    total,
    peak,
    slot_a,
    m_a,
    l_a,
    acc,
    slot_b,
    o_send,
    s_pair,
    s_q,
    r_q,
    s_kv,
    r_kv,
    s_fwd,
    s_o,
    r_o,
    s_own,
):
    me = lax.axis_index("seq")
    core, chip = me % 2, me // 2
    partner = chip * 2 + 1 - core
    kv = (kv_a, kv_b)
    qi, k1, k2, pairs, first, la, last = [lists.at[i] for i in range(7)]

    def remote(src, dst, send, recv, device):
        return pltpu.make_async_remote_copy(
            src_ref=src, dst_ref=dst, send_sem=send, recv_sem=recv, device_id={"seq": device}, device_id_type=MESH
        )

    def cols(head):
        return pl.ds(pl.multiple_of(head * HD, HD), HD)

    def pair_load(head):
        return pltpu.make_async_copy(kv_hbm.at[:, :, cols(head)], pair.at[head], s_pair.at[head])

    def pair_loads(n, _):
        pair_load(chip_at(chip, n, core)).start()
        return 0

    lax.fori_loop(0, CHIPS, pair_loads, 0)

    barrier = pltpu.get_barrier_semaphore()
    for d in range(1, DEVS):
        pl.semaphore_signal(barrier, inc=1, device_id={"seq": (me + d) % DEVS}, device_id_type=MESH)
    pl.semaphore_wait(barrier, DEVS - 1)

    def q_copy(jj):
        device = target(me, jj)
        rows = pl.ds(pl.multiple_of((device % 2) * HALF, HALF), HALF)
        return remote(q_hbm.at[rows, cols(device // 2)], q.at[me], s_q.at[jj], r_q.at[me], device)

    def q_sends(jj, _):
        q_copy(jj).start()
        return 0

    lax.fori_loop(0, DEVS - 1, q_sends, 0)
    own_rows = pl.ds(pl.multiple_of(core * HALF, HALF), HALF)
    own_q = pltpu.make_async_copy(q_hbm.at[own_rows, cols(chip)], q.at[me], s_own.at[0])
    own_q.start()

    def kv_copy(u, n):
        t = chip_at(chip, n, core)
        return remote(stage.at[t, u], kv[u].at[me], s_kv.at[u, n], r_kv.at[u, me], t * 2 + core)

    def split(n, _):
        t = chip_at(chip, n, core)
        pair_load(t).wait()
        wide[...] = pair[t].reshape(2 * 2 * HALF, HD).astype(jnp.float32)
        keys = wide[pl.ds(0, 2 * HALF, stride=2), :].astype(jnp.bfloat16)
        values = wide[pl.ds(1, 2 * HALF, stride=2), :].T.astype(jnp.bfloat16)
        for u in range(2):
            stage[t, u, 0:HALF] = keys[u * HALF : (u + 1) * HALF]
            stage[t, u, HALF : HALF + HD] = values[:, u * HALF : u * HALF + HD]
            stage[t, u, HALF + HD : 2 * HALF] = values[:, u * HALF + HD : (u + 1) * HALF]

        @pl.when(n < CHIPS - 1)
        def _():
            kv_copy(0, n).start()

        return 0

    lax.fori_loop(0, CHIPS, split, 0)

    def kv_sends(n, _):
        kv_copy(1, n).start()
        return 0

    lax.fori_loop(0, CHIPS - 1, kv_sends, 0)
    own_kv = [pltpu.make_async_copy(stage.at[chip, u], kv[u].at[me], s_own.at[1 + u]) for u in range(2)]
    own_fwd = [
        remote(stage.at[chip, u], kv[u].at[me], s_fwd.at[u, CHIPS - 1], r_kv.at[u, me], partner) for u in range(2)
    ]
    for u in range(2):
        own_kv[u].start()
        own_fwd[u].start()

    def forward_copy(u, n):
        p = chip_at(chip, n, core, -1) * 2 + core
        return remote(kv[u].at[p], kv[u].at[p], s_fwd.at[u, n], r_kv.at[u, p], partner)

    def forward(u):
        def step(n, _):
            copy = forward_copy(u, n)
            copy.wait_recv()
            copy.start()
            return 0

        return step

    def kv_arrive(u):
        def step(c, _):
            p = c * 2 + 1 - core
            remote(kv[u].at[p], kv[u].at[p], s_fwd.at[u, 0], r_kv.at[u, p], partner).wait_recv()
            return 0

        lax.fori_loop(0, CHIPS, step, 0)

    def q_arrive(d, _):
        p = (me + d) % DEVS
        remote(q.at[p], q.at[p], s_q.at[0], r_q.at[p], partner).wait_recv()
        return 0

    lax.fori_loop(1, DEVS, q_arrive, 0)
    own_q.wait()

    def turn(p, _):
        q_t[p] = q[p].T
        return 0

    lax.fori_loop(0, DEVS, turn, 0)
    lax.fori_loop(0, CHIPS - 1, forward(0), 0)
    own_kv[0].wait()
    kv_arrive(0)

    def stage_scores(u, s, w):
        keys = jnp.concatenate([kv[u][k1[s], 0:HALF], kv[u][k2[s], 0:HALF]], axis=0)
        sc = dot_nn(keys, q_t[qi[s]])
        scores[w] = sc
        one = jnp.max(sc[0:HALF], axis=0, keepdims=True)
        two = jnp.max(sc[HALF : 2 * HALF], axis=0, keepdims=True)
        peak[w] = jnp.where(pairs[s] == 1, jnp.maximum(one, two), one) * SCALE

    def stage_weights(u, s, w, carry):
        m, l = carry
        new = first[s] == 1
        m = jnp.where(new, LOW if u == 0 else m_a[la[s]], m)
        l = jnp.where(new, 0.0 if u == 0 else l_a[la[s]], l)
        m_new = jnp.maximum(m, peak[w])
        m_two = jnp.where(pairs[s] == 1, m_new, -LOW)
        al = jnp.exp2(m - m_new)
        l = l * al
        for x, m_x in enumerate((m_new, m_two)):
            rows = pl.ds(x * HALF, HALF)
            p = jnp.exp2(scores[w, rows] * SCALE - m_x)
            l = l + jnp.sum(p, axis=0, keepdims=True)
            probs[w, rows] = p.astype(jnp.bfloat16)
        alpha[w] = al
        if u == 0:
            m_a[s] = m_new
            l_a[s] = l
        else:
            total[w] = l
        return m_new, l

    def stage_values(u, s, w):
        blocks = [kv[u][k[s], HALF + x * HD : HALF + (x + 1) * HD] for k in (k1, k2) for x in range(2)]
        d = dot_nn(jnp.concatenate(blocks, axis=1), probs[w])
        prev = acc[...]
        if u == 1:
            prev = jnp.where(first[s] == 1, slot_a[la[s]], prev)
        a = prev * alpha[w] + d
        acc[...] = a
        if u == 0:
            slot_a[s] = a
        else:
            slot_b[s] = (a * (1.0 / total[w])).astype(jnp.bfloat16)

    def attend(u, beside):
        ahead_s, ahead_w = 4, 2
        acc[...] = jnp.zeros_like(acc)
        carry = (jnp.zeros((1, HALF), jnp.float32), jnp.zeros((1, HALF), jnp.float32))
        for s in range(ahead_s):
            stage_scores(u, s, s)
        for s in range(ahead_w):
            carry = stage_weights(u, s, s, carry)

        def body(t, carry):
            for w in range(UNROLL):
                s = t * UNROLL + w
                stage_values(u, s, w)
                stage_scores(u, s + ahead_s, (w + ahead_s) % UNROLL)
                carry = stage_weights(u, s + ahead_w, (w + ahead_w) % UNROLL, carry)
            beside(t)
            return carry

        lax.fori_loop(0, UNITS // UNROLL, body, carry)

    def forwards_due(t):
        return jnp.clip(t - 2, 0, CHIPS - 1)

    def beside_a(t):
        lax.fori_loop(forwards_due(t), forwards_due(t + 1), forward(1), 0)

    attend(0, beside_a)
    lax.fori_loop(UNITS // UNROLL - 2, CHIPS - 1, forward(1), 0)
    own_kv[1].wait()
    kv_arrive(1)

    def o_copy(jj):
        out_rows = pl.ds(pl.multiple_of(core * HALF, HALF), HALF)
        return remote(o_send.at[jj], out_hbm.at[out_rows, cols(chip)], s_o.at[jj], r_o.at[me], target(me, jj))

    own_o = pltpu.make_async_copy(o_send.at[DEVS - 1], out_hbm.at[own_rows, cols(chip)], s_own.at[3])

    def emit(jj, _):
        o_send[jj] = slot_b[last[jj]].astype(jnp.float32).T.astype(jnp.bfloat16)

        @pl.when(jj < DEVS - 1)
        def _():
            o_copy(jj).start()

        @pl.when(jj == DEVS - 1)
        def _():
            own_o.start()

        return 0

    def outputs_due(t):
        s = t * UNROLL
        return jnp.clip(jnp.maximum(s // MAX_UNITS, s - (MOST - DEVS)), 0, DEVS)

    def beside_b(t):
        lax.fori_loop(outputs_due(t), outputs_due(t + 1), emit, 0)

    attend(1, beside_b)

    def q_sent(jj, _):
        q_copy(jj).wait_send()
        return 0

    lax.fori_loop(0, DEVS - 1, q_sent, 0)
    for u in range(2):

        def kv_sent(n, _, u=u):
            kv_copy(u, n).wait_send()
            forward_copy(u, n).wait_send()
            return 0

        lax.fori_loop(0, CHIPS - 1, kv_sent, 0)
        own_fwd[u].wait_send()

    def o_sent(jj, _):
        o_copy(jj).wait_send()
        return 0

    lax.fori_loop(0, DEVS - 1, o_sent, 0)
    own_o.wait()

    def o_arrive(d, _):
        p = (me + d) % DEVS
        rows = pl.ds(pl.multiple_of((p % 2) * HALF, HALF), HALF)
        remote(o_send.at[0], out_hbm.at[rows, cols(p // 2)], s_o.at[0], r_o.at[p], partner).wait_recv()
        return 0

    lax.fori_loop(1, DEVS, o_arrive, 0)


def local(queries, keys_values, image_tiles, loader_tiles):
    bf16, f32 = jnp.bfloat16, jnp.float32
    anywhere = pl.BlockSpec(memory_space=pl.ANY)
    smem = pl.BlockSpec(memory_space=pltpu.SMEM)
    dma = pltpu.SemaphoreType.DMA

    vmem = pl.BlockSpec(memory_space=pltpu.VMEM)
    lists = pl.pallas_call(
        list_kernel,
        out_shape=jax.ShapeDtypeStruct((8, LISTS), jnp.int32),
        in_specs=[smem] * 2,
        out_specs=vmem,
        name="lists",
    )(image_tiles, loader_tiles)
    return pl.pallas_call(
        attend_kernel,
        out_shape=jax.ShapeDtypeStruct(queries.shape, bf16),
        in_specs=[anywhere] * 2 + [smem],
        out_specs=anywhere,
        scratch_shapes=[
            pltpu.VMEM((CHIPS, 2 * HALF, 2, HD), bf16),
            pltpu.VMEM((4 * HALF, HD), f32),
            pltpu.VMEM((CHIPS, 2, 2 * HALF, HD), bf16),
            pltpu.VMEM((DEVS, 2 * HALF, HD), bf16),
            pltpu.VMEM((DEVS, 2 * HALF, HD), bf16),
            pltpu.VMEM((DEVS, HALF, HD), bf16),
            pltpu.VMEM((DEVS, HD, HALF), bf16),
            pltpu.VMEM((UNROLL, 2 * HALF, HALF), f32),
            pltpu.VMEM((UNROLL, 2 * HALF, HALF), bf16),
            pltpu.VMEM((UNROLL, 1, HALF), f32),
            pltpu.VMEM((UNROLL, 1, HALF), f32),
            pltpu.VMEM((UNROLL, 1, HALF), f32),
            pltpu.VMEM((UNITS, HD, HALF), f32),
            pltpu.VMEM((LISTS, 1, HALF), f32),
            pltpu.VMEM((LISTS, 1, HALF), f32),
            pltpu.VMEM((HD, HALF), f32),
            pltpu.VMEM((UNITS, HD, HALF), bf16),
            pltpu.VMEM((DEVS, HALF, HD), bf16),
            dma((CHIPS,)),
            dma((DEVS,)),
            dma((DEVS,)),
            dma((2, CHIPS)),
            dma((2, DEVS)),
            dma((2, CHIPS)),
            dma((DEVS,)),
            dma((DEVS,)),
            dma((4,)),
        ],
        compiler_params=pltpu.CompilerParams(collective_id=0, has_side_effects=True, vmem_limit_bytes=48 << 20),
        name="attend",
    )(queries, keys_values, lists)


def solution(mesh):
    in_specs = (P(("dp", "seq"), None), P(("dp", "seq"), None, None), P("dp"), P("dp"))
    out_specs = P(("dp", "seq"), None)
    return jax.shard_map(local, mesh=mesh, in_specs=in_specs, out_specs=out_specs, check_vma=False)
```

```python
import functools

import jax
import jax.numpy as jnp
from jax import lax
from jax.experimental import pallas as pl
from jax.experimental.pallas import tpu as pltpu
from jax.sharding import PartitionSpec as P

MESH = pl.DeviceIdType.MESH
HD = 128
HALF = 256
SIDE = 4
CHIPS = 16
DEVS = 32
MAX_UNITS = 4
UNITS = 84
MOST = 83
UNROLL = 6
LISTS = 128
SCALE = HD**-0.5 * 1.4426950408889634
LOW = -1e30


ORDER = ((2, 0), (0, 2), (2, 1), (2, 3), (1, 2), (3, 2), (2, 2), (1, 0), (3, 0), (0, 1), (0, 3), (1, 1), (3, 3), (1, 3), (3, 1))


def offset(n, core):
    a, b = jnp.zeros_like(n), jnp.zeros_like(n)
    for k, (along_z, along_x) in enumerate(ORDER):
        a = jnp.where(n == k, along_z, a)
        b = jnp.where(n == k, along_x, b)
    return jnp.where(core == 0, a, b), jnp.where(core == 0, b, a)


def chip_at(chip, n, core, sign=1):
    dz, dx = offset(n, core)
    z, x = chip // SIDE, chip % SIDE
    return ((z + SIDE + sign * dz) % SIDE) * SIDE + (x + SIDE + sign * dx) % SIDE


def target(me, jj):
    core, chip = me % 2, me // 2
    n, e = jj // 2, jj % 2
    return chip_at(chip, n, core) * 2 + (core + 1 - e) % 2


def list_kernel(tiles_ref, loader_ref, lists_ref):
    me = lax.axis_index("seq")
    f32 = jnp.float32
    images = tiles_ref.shape[0]

    def grid(shape, axis):
        return lax.broadcasted_iota(jnp.int32, shape, axis)

    def pick(mask, values, axis):
        return jnp.sum(jnp.where(mask, values, 0.0), axis=axis, keepdims=True)

    def across(ref):
        n = ref.shape[0]
        values = jnp.zeros((1, n), jnp.int32)
        for i in range(n):
            values = jnp.where(grid((1, n), 1) == i, ref[i], values)
        return values.astype(f32)

    tiles, loader = across(tiles_ref), across(loader_ref)
    row, col = grid((DEVS, DEVS), 0), grid((DEVS, DEVS), 1)
    image_row, image_col = grid((images, images), 0), grid((images, images), 1)
    loader_down = pick(row == col, loader, 1)
    tiles_down = pick(image_row == image_col, tiles, 1)
    ends = pick(image_row <= image_col, tiles_down, 0)
    starts = ends - tiles
    place = target(me, grid((DEVS, 1), 0))
    tile = pick(place == col, loader, 1)
    lo, hi = pick(ends <= tile, tiles, 1), pick(starts <= tile, tiles, 1)
    count = jnp.floor((hi - lo + 1.0) * 0.5)
    after = pick(col <= row, pick(row == col, count, 0), 1)
    before = after - count
    s = grid((1, LISTS), 1).astype(f32)
    mine = (before <= s) & (s < after)
    r = s - pick(mine, before, 0)
    one = pick(mine, lo, 0) + 2.0 * r
    two = jnp.minimum(one + 1.0, pick(mine, hi, 0) - 1.0)
    down = grid((DEVS, LISTS), 0)
    devices = down.astype(f32)
    live = s < jnp.sum(count, axis=0, keepdims=True)
    lists = (
        pick(mine, place.astype(f32), 0),
        pick(loader_down == one, devices, 0),
        pick(loader_down == two, devices, 0),
        jnp.where(live, two - one, 0.0),
        jnp.where(live, jnp.where(r == 0.0, 1.0, 0.0), 1.0),
        pick(mine, after - 1.0, 0),
        pick(down == grid((DEVS, LISTS), 1), after - 1.0, 0),
    )
    for i, values in enumerate(lists):
        lists_ref[i : i + 1, :] = values.astype(jnp.int32)
    lists_ref[len(lists) : len(lists) + 1, :] = jnp.zeros((1, LISTS), jnp.int32)


def dot_nn(a, b):
    return lax.dot_general(a, b, (((1,), (0,)), ((), ())), preferred_element_type=jnp.float32)


def attend_kernel(
    q_hbm,
    kv_hbm,
    lists,
    out_hbm,
    pair,
    wide,
    stage,
    kv_a,
    kv_b,
    q,
    q_t,
    scores,
    probs,
    alpha,
    total,
    peak,
    slot_a,
    m_a,
    l_a,
    acc,
    slot_b,
    o_send,
    s_pair,
    s_q,
    r_q,
    s_kv,
    r_kv,
    s_fwd,
    s_o,
    r_o,
    s_own,
):
    me = lax.axis_index("seq")
    core, chip = me % 2, me // 2
    partner = chip * 2 + 1 - core
    kv = (kv_a, kv_b)
    qi, k1, k2, pairs, first, la, last = [lists.at[i] for i in range(7)]

    def remote(src, dst, send, recv, device):
        return pltpu.make_async_remote_copy(
            src_ref=src, dst_ref=dst, send_sem=send, recv_sem=recv, device_id={"seq": device}, device_id_type=MESH
        )

    def cols(head):
        return pl.ds(pl.multiple_of(head * HD, HD), HD)

    def pair_load(head):
        return pltpu.make_async_copy(kv_hbm.at[:, :, cols(head)], pair.at[head], s_pair.at[head])

    def pair_loads(n, _):
        pair_load(chip_at(chip, n, core)).start()
        return 0

    lax.fori_loop(0, CHIPS, pair_loads, 0)

    barrier = pltpu.get_barrier_semaphore()
    for d in range(1, DEVS):
        pl.semaphore_signal(barrier, inc=1, device_id={"seq": (me + d) % DEVS}, device_id_type=MESH)
    pl.semaphore_wait(barrier, DEVS - 1)

    def q_copy(jj):
        device = target(me, jj)
        rows = pl.ds(pl.multiple_of((device % 2) * HALF, HALF), HALF)
        return remote(q_hbm.at[rows, cols(device // 2)], q.at[me], s_q.at[jj], r_q.at[me], device)

    def q_sends(jj, _):
        q_copy(jj).start()
        return 0

    lax.fori_loop(0, DEVS - 1, q_sends, 0)
    own_rows = pl.ds(pl.multiple_of(core * HALF, HALF), HALF)
    own_q = pltpu.make_async_copy(q_hbm.at[own_rows, cols(chip)], q.at[me], s_own.at[0])
    own_q.start()

    def kv_copy(u, n):
        t = chip_at(chip, n, core)
        return remote(stage.at[t, u], kv[u].at[me], s_kv.at[u, n], r_kv.at[u, me], t * 2 + core)

    def split(n, _):
        t = chip_at(chip, n, core)
        pair_load(t).wait()
        wide[...] = pair[t].reshape(2 * 2 * HALF, HD).astype(jnp.float32)
        keys = wide[pl.ds(0, 2 * HALF, stride=2), :].astype(jnp.bfloat16)
        values = wide[pl.ds(1, 2 * HALF, stride=2), :].T.astype(jnp.bfloat16)
        for u in range(2):
            stage[t, u, 0:HALF] = keys[u * HALF : (u + 1) * HALF]
            stage[t, u, HALF : HALF + HD] = values[:, u * HALF : u * HALF + HD]
            stage[t, u, HALF + HD : 2 * HALF] = values[:, u * HALF + HD : (u + 1) * HALF]

        @pl.when(n < CHIPS - 1)
        def _():
            kv_copy(0, n).start()

        return 0

    lax.fori_loop(0, CHIPS, split, 0)

    def kv_sends(n, _):
        kv_copy(1, n).start()
        return 0

    lax.fori_loop(0, CHIPS - 1, kv_sends, 0)
    own_kv = [pltpu.make_async_copy(stage.at[chip, u], kv[u].at[me], s_own.at[1 + u]) for u in range(2)]
    own_fwd = [
        remote(stage.at[chip, u], kv[u].at[me], s_fwd.at[u, CHIPS - 1], r_kv.at[u, me], partner) for u in range(2)
    ]
    for u in range(2):
        own_kv[u].start()
        own_fwd[u].start()

    def forward_copy(u, n):
        p = chip_at(chip, n, core, -1) * 2 + core
        return remote(kv[u].at[p], kv[u].at[p], s_fwd.at[u, n], r_kv.at[u, p], partner)

    def forward(u):
        def step(n, _):
            copy = forward_copy(u, n)
            copy.wait_recv()
            copy.start()
            return 0

        return step

    def kv_arrive(u):
        def step(c, _):
            p = c * 2 + 1 - core
            remote(kv[u].at[p], kv[u].at[p], s_fwd.at[u, 0], r_kv.at[u, p], partner).wait_recv()
            return 0

        lax.fori_loop(0, CHIPS, step, 0)

    def q_arrive(d, _):
        p = (me + d) % DEVS
        remote(q.at[p], q.at[p], s_q.at[0], r_q.at[p], partner).wait_recv()
        return 0

    lax.fori_loop(1, DEVS, q_arrive, 0)
    own_q.wait()

    def turn(p, _):
        q_t[p] = q[p].T
        return 0

    lax.fori_loop(0, DEVS, turn, 0)
    lax.fori_loop(0, CHIPS - 1, forward(0), 0)
    own_kv[0].wait()
    kv_arrive(0)

    def stage_scores(u, s, w):
        keys = jnp.concatenate([kv[u][k1[s], 0:HALF], kv[u][k2[s], 0:HALF]], axis=0)
        sc = dot_nn(keys, q_t[qi[s]])
        scores[w] = sc
        one = jnp.max(sc[0:HALF], axis=0, keepdims=True)
        two = jnp.max(sc[HALF : 2 * HALF], axis=0, keepdims=True)
        peak[w] = jnp.where(pairs[s] == 1, jnp.maximum(one, two), one) * SCALE

    def stage_weights(u, s, w, carry):
        m, l = carry
        new = first[s] == 1
        m = jnp.where(new, LOW if u == 0 else m_a[la[s]], m)
        l = jnp.where(new, 0.0 if u == 0 else l_a[la[s]], l)
        m_new = jnp.maximum(m, peak[w])
        m_two = jnp.where(pairs[s] == 1, m_new, -LOW)
        al = jnp.exp2(m - m_new)
        l = l * al
        for x, m_x in enumerate((m_new, m_two)):
            rows = pl.ds(x * HALF, HALF)
            p = jnp.exp2(scores[w, rows] * SCALE - m_x)
            l = l + jnp.sum(p, axis=0, keepdims=True)
            probs[w, rows] = p.astype(jnp.bfloat16)
        alpha[w] = al
        if u == 0:
            m_a[s] = m_new
            l_a[s] = l
        else:
            total[w] = l
        return m_new, l

    def stage_values(u, s, w):
        blocks = [kv[u][k[s], HALF + x * HD : HALF + (x + 1) * HD] for k in (k1, k2) for x in range(2)]
        d = dot_nn(jnp.concatenate(blocks, axis=1), probs[w])
        prev = acc[...]
        if u == 1:
            prev = jnp.where(first[s] == 1, slot_a[la[s]], prev)
        a = prev * alpha[w] + d
        acc[...] = a
        if u == 0:
            slot_a[s] = a
        else:
            slot_b[s] = (a * (1.0 / total[w])).T.astype(jnp.bfloat16)

    def attend(u, beside):
        ahead_s, ahead_w = 4, 2
        acc[...] = jnp.zeros_like(acc)
        carry = (jnp.zeros((1, HALF), jnp.float32), jnp.zeros((1, HALF), jnp.float32))
        for s in range(ahead_s):
            stage_scores(u, s, s)
        for s in range(ahead_w):
            carry = stage_weights(u, s, s, carry)

        def body(t, carry):
            for w in range(UNROLL):
                s = t * UNROLL + w
                stage_values(u, s, w)
                stage_scores(u, s + ahead_s, (w + ahead_s) % UNROLL)
                carry = stage_weights(u, s + ahead_w, (w + ahead_w) % UNROLL, carry)
            beside(t)
            return carry

        lax.fori_loop(0, UNITS // UNROLL, body, carry)

    def forwards_due(t):
        return jnp.clip(t - 2, 0, CHIPS - 1)

    def beside_a(t):
        lax.fori_loop(forwards_due(t), forwards_due(t + 1), forward(1), 0)

    attend(0, beside_a)
    lax.fori_loop(UNITS // UNROLL - 2, CHIPS - 1, forward(1), 0)
    own_kv[1].wait()
    kv_arrive(1)

    def o_copy(jj):
        out_rows = pl.ds(pl.multiple_of(core * HALF, HALF), HALF)
        return remote(o_send.at[jj], out_hbm.at[out_rows, cols(chip)], s_o.at[jj], r_o.at[me], target(me, jj))

    own_o = pltpu.make_async_copy(o_send.at[DEVS - 1], out_hbm.at[own_rows, cols(chip)], s_own.at[3])

    def emit(jj, _):
        o_send[jj] = slot_b[last[jj]]

        @pl.when(jj < DEVS - 1)
        def _():
            o_copy(jj).start()

        @pl.when(jj == DEVS - 1)
        def _():
            own_o.start()

        return 0

    def outputs_due(t):
        s = t * UNROLL
        return jnp.clip(jnp.maximum(s // MAX_UNITS, s - (MOST - DEVS)), 0, DEVS)

    def beside_b(t):
        lax.fori_loop(outputs_due(t), outputs_due(t + 1), emit, 0)

    attend(1, beside_b)

    def q_sent(jj, _):
        q_copy(jj).wait_send()
        return 0

    lax.fori_loop(0, DEVS - 1, q_sent, 0)
    for u in range(2):

        def kv_sent(n, _, u=u):
            kv_copy(u, n).wait_send()
            forward_copy(u, n).wait_send()
            return 0

        lax.fori_loop(0, CHIPS - 1, kv_sent, 0)
        own_fwd[u].wait_send()

    def o_sent(jj, _):
        o_copy(jj).wait_send()
        return 0

    lax.fori_loop(0, DEVS - 1, o_sent, 0)
    own_o.wait()

    def o_arrive(d, _):
        p = (me + d) % DEVS
        rows = pl.ds(pl.multiple_of((p % 2) * HALF, HALF), HALF)
        remote(o_send.at[0], out_hbm.at[rows, cols(p // 2)], s_o.at[0], r_o.at[p], partner).wait_recv()
        return 0

    lax.fori_loop(1, DEVS, o_arrive, 0)


def local(queries, keys_values, image_tiles, loader_tiles):
    bf16, f32 = jnp.bfloat16, jnp.float32
    anywhere = pl.BlockSpec(memory_space=pl.ANY)
    smem = pl.BlockSpec(memory_space=pltpu.SMEM)
    dma = pltpu.SemaphoreType.DMA

    vmem = pl.BlockSpec(memory_space=pltpu.VMEM)
    lists = pl.pallas_call(
        list_kernel,
        out_shape=jax.ShapeDtypeStruct((8, LISTS), jnp.int32),
        in_specs=[smem] * 2,
        out_specs=vmem,
        name="lists",
    )(image_tiles, loader_tiles)
    return pl.pallas_call(
        attend_kernel,
        out_shape=jax.ShapeDtypeStruct(queries.shape, bf16),
        in_specs=[anywhere] * 2 + [smem],
        out_specs=anywhere,
        scratch_shapes=[
            pltpu.VMEM((CHIPS, 2 * HALF, 2, HD), bf16),
            pltpu.VMEM((4 * HALF, HD), f32),
            pltpu.VMEM((CHIPS, 2, 2 * HALF, HD), bf16),
            pltpu.VMEM((DEVS, 2 * HALF, HD), bf16),
            pltpu.VMEM((DEVS, 2 * HALF, HD), bf16),
            pltpu.VMEM((DEVS, HALF, HD), bf16),
            pltpu.VMEM((DEVS, HD, HALF), bf16),
            pltpu.VMEM((UNROLL, 2 * HALF, HALF), f32),
            pltpu.VMEM((UNROLL, 2 * HALF, HALF), bf16),
            pltpu.VMEM((UNROLL, 1, HALF), f32),
            pltpu.VMEM((UNROLL, 1, HALF), f32),
            pltpu.VMEM((UNROLL, 1, HALF), f32),
            pltpu.VMEM((UNITS, HD, HALF), f32),
            pltpu.VMEM((LISTS, 1, HALF), f32),
            pltpu.VMEM((LISTS, 1, HALF), f32),
            pltpu.VMEM((HD, HALF), f32),
            pltpu.VMEM((UNITS, HALF, HD), bf16),
            pltpu.VMEM((DEVS, HALF, HD), bf16),
            dma((CHIPS,)),
            dma((DEVS,)),
            dma((DEVS,)),
            dma((2, CHIPS)),
            dma((2, DEVS)),
            dma((2, CHIPS)),
            dma((DEVS,)),
            dma((DEVS,)),
            dma((4,)),
        ],
        compiler_params=pltpu.CompilerParams(collective_id=0, has_side_effects=True, vmem_limit_bytes=51 << 20),
        name="attend",
    )(queries, keys_values, lists)


def solution(mesh):
    in_specs = (P(("dp", "seq"), None), P(("dp", "seq"), None, None), P("dp"), P("dp"))
    out_specs = P(("dp", "seq"), None)
    return jax.shard_map(local, mesh=mesh, in_specs=in_specs, out_specs=out_specs, check_vma=False)
```

```python
import functools

import jax
import jax.numpy as jnp
from jax import lax
from jax.experimental import pallas as pl
from jax.experimental.pallas import tpu as pltpu
from jax.sharding import PartitionSpec as P

MESH = pl.DeviceIdType.MESH
HD = 128
HALF = 256
SIDE = 4
CHIPS = 16
DEVS = 32
MAX_UNITS = 4
UNITS = 84
MOST = 83
UNROLL = 6
LISTS = 128
SCALE = HD**-0.5 * 1.4426950408889634
LOW = -1e30


ORDER = ((2, 2), (2, 1), (2, 3), (1, 2), (3, 2), (2, 0), (0, 2), (1, 1), (3, 3), (1, 3), (3, 1), (1, 0), (3, 0), (0, 1), (0, 3))


def offset(n, core):
    a, b = jnp.zeros_like(n), jnp.zeros_like(n)
    for k, (along_z, along_x) in enumerate(ORDER):
        a = jnp.where(n == k, along_z, a)
        b = jnp.where(n == k, along_x, b)
    return jnp.where(core == 0, a, b), jnp.where(core == 0, b, a)


def chip_at(chip, n, core, sign=1):
    dz, dx = offset(n, core)
    z, x = chip // SIDE, chip % SIDE
    return ((z + SIDE + sign * dz) % SIDE) * SIDE + (x + SIDE + sign * dx) % SIDE


def target(me, jj):
    core, chip = me % 2, me // 2
    n, e = jj // 2, jj % 2
    return chip_at(chip, n, core) * 2 + (core + 1 - e) % 2


def list_kernel(tiles_ref, loader_ref, lists_ref):
    me = lax.axis_index("seq")
    f32 = jnp.float32
    images = tiles_ref.shape[0]

    def grid(shape, axis):
        return lax.broadcasted_iota(jnp.int32, shape, axis)

    def pick(mask, values, axis):
        return jnp.sum(jnp.where(mask, values, 0.0), axis=axis, keepdims=True)

    def across(ref):
        n = ref.shape[0]
        values = jnp.zeros((1, n), jnp.int32)
        for i in range(n):
            values = jnp.where(grid((1, n), 1) == i, ref[i], values)
        return values.astype(f32)

    tiles, loader = across(tiles_ref), across(loader_ref)
    row, col = grid((DEVS, DEVS), 0), grid((DEVS, DEVS), 1)
    image_row, image_col = grid((images, images), 0), grid((images, images), 1)
    loader_down = pick(row == col, loader, 1)
    tiles_down = pick(image_row == image_col, tiles, 1)
    ends = pick(image_row <= image_col, tiles_down, 0)
    starts = ends - tiles
    place = target(me, grid((DEVS, 1), 0))
    tile = pick(place == col, loader, 1)
    lo, hi = pick(ends <= tile, tiles, 1), pick(starts <= tile, tiles, 1)
    count = jnp.floor((hi - lo + 1.0) * 0.5)
    after = pick(col <= row, pick(row == col, count, 0), 1)
    before = after - count
    s = grid((1, LISTS), 1).astype(f32)
    mine = (before <= s) & (s < after)
    r = s - pick(mine, before, 0)
    one = pick(mine, lo, 0) + 2.0 * r
    two = jnp.minimum(one + 1.0, pick(mine, hi, 0) - 1.0)
    down = grid((DEVS, LISTS), 0)
    devices = down.astype(f32)
    live = s < jnp.sum(count, axis=0, keepdims=True)
    lists = (
        pick(mine, place.astype(f32), 0),
        pick(loader_down == one, devices, 0),
        pick(loader_down == two, devices, 0),
        jnp.where(live, two - one, 0.0),
        jnp.where(live, jnp.where(r == 0.0, 1.0, 0.0), 1.0),
        pick(mine, after - 1.0, 0),
        pick(down == grid((DEVS, LISTS), 1), after - 1.0, 0),
    )
    for i, values in enumerate(lists):
        lists_ref[i : i + 1, :] = values.astype(jnp.int32)
    lists_ref[len(lists) : len(lists) + 1, :] = jnp.zeros((1, LISTS), jnp.int32)


def dot_nn(a, b):
    return lax.dot_general(a, b, (((1,), (0,)), ((), ())), preferred_element_type=jnp.float32)


def attend_kernel(
    q_hbm,
    kv_hbm,
    lists,
    out_hbm,
    pair,
    wide,
    stage,
    kv_a,
    kv_b,
    q,
    q_t,
    scores,
    probs,
    alpha,
    total,
    peak,
    slot_a,
    m_a,
    l_a,
    acc,
    slot_b,
    o_send,
    s_pair,
    s_q,
    r_q,
    s_kv,
    r_kv,
    s_fwd,
    s_o,
    r_o,
    s_own,
):
    me = lax.axis_index("seq")
    core, chip = me % 2, me // 2
    partner = chip * 2 + 1 - core
    kv = (kv_a, kv_b)
    qi, k1, k2, pairs, first, la, last = [lists.at[i] for i in range(7)]

    def remote(src, dst, send, recv, device):
        return pltpu.make_async_remote_copy(
            src_ref=src, dst_ref=dst, send_sem=send, recv_sem=recv, device_id={"seq": device}, device_id_type=MESH
        )

    def cols(head):
        return pl.ds(pl.multiple_of(head * HD, HD), HD)

    def pair_load(head):
        return pltpu.make_async_copy(kv_hbm.at[:, :, cols(head)], pair.at[head], s_pair.at[head])

    def pair_loads(n, _):
        pair_load(chip_at(chip, n, core)).start()
        return 0

    lax.fori_loop(0, CHIPS, pair_loads, 0)

    barrier = pltpu.get_barrier_semaphore()
    for d in range(1, DEVS):
        pl.semaphore_signal(barrier, inc=1, device_id={"seq": (me + d) % DEVS}, device_id_type=MESH)
    pl.semaphore_wait(barrier, DEVS - 1)

    def q_copy(jj):
        device = target(me, jj)
        rows = pl.ds(pl.multiple_of((device % 2) * HALF, HALF), HALF)
        return remote(q_hbm.at[rows, cols(device // 2)], q.at[me], s_q.at[jj], r_q.at[me], device)

    def q_sends(jj, _):
        q_copy(jj).start()
        return 0

    lax.fori_loop(0, DEVS - 1, q_sends, 0)
    own_rows = pl.ds(pl.multiple_of(core * HALF, HALF), HALF)
    own_q = pltpu.make_async_copy(q_hbm.at[own_rows, cols(chip)], q.at[me], s_own.at[0])
    own_q.start()

    def kv_copy(u, n):
        t = chip_at(chip, n, core)
        return remote(stage.at[t, u], kv[u].at[me], s_kv.at[u, n], r_kv.at[u, me], t * 2 + core)

    def split(n, _):
        t = chip_at(chip, n, core)
        pair_load(t).wait()
        wide[...] = pair[t].reshape(2 * 2 * HALF, HD).astype(jnp.float32)
        keys = wide[pl.ds(0, 2 * HALF, stride=2), :].astype(jnp.bfloat16)
        values = wide[pl.ds(1, 2 * HALF, stride=2), :].T.astype(jnp.bfloat16)
        for u in range(2):
            stage[t, u, 0:HALF] = keys[u * HALF : (u + 1) * HALF]
            stage[t, u, HALF : HALF + HD] = values[:, u * HALF : u * HALF + HD]
            stage[t, u, HALF + HD : 2 * HALF] = values[:, u * HALF + HD : (u + 1) * HALF]

        @pl.when(n < CHIPS - 1)
        def _():
            kv_copy(0, n).start()

        return 0

    lax.fori_loop(0, CHIPS, split, 0)

    def kv_sends(n, _):
        kv_copy(1, n).start()
        return 0

    lax.fori_loop(0, CHIPS - 1, kv_sends, 0)
    own_kv = [pltpu.make_async_copy(stage.at[chip, u], kv[u].at[me], s_own.at[1 + u]) for u in range(2)]
    own_fwd = [
        remote(stage.at[chip, u], kv[u].at[me], s_fwd.at[u, CHIPS - 1], r_kv.at[u, me], partner) for u in range(2)
    ]
    for u in range(2):
        own_kv[u].start()
        own_fwd[u].start()

    def forward_copy(u, n):
        p = chip_at(chip, n, core, -1) * 2 + core
        return remote(kv[u].at[p], kv[u].at[p], s_fwd.at[u, n], r_kv.at[u, p], partner)

    def forward(u):
        def step(n, _):
            copy = forward_copy(u, n)
            copy.wait_recv()
            copy.start()
            return 0

        return step

    def kv_arrive(u):
        def step(c, _):
            p = c * 2 + 1 - core
            remote(kv[u].at[p], kv[u].at[p], s_fwd.at[u, 0], r_kv.at[u, p], partner).wait_recv()
            return 0

        lax.fori_loop(0, CHIPS, step, 0)

    def q_arrive(d, _):
        p = (me + d) % DEVS
        remote(q.at[p], q.at[p], s_q.at[0], r_q.at[p], partner).wait_recv()
        return 0

    lax.fori_loop(1, DEVS, q_arrive, 0)
    own_q.wait()

    def turn(p, _):
        q_t[p] = q[p].T
        return 0

    lax.fori_loop(0, DEVS, turn, 0)
    lax.fori_loop(0, CHIPS - 1, forward(0), 0)
    own_kv[0].wait()
    kv_arrive(0)

    def stage_scores(u, s, w):
        keys = jnp.concatenate([kv[u][k1[s], 0:HALF], kv[u][k2[s], 0:HALF]], axis=0)
        sc = dot_nn(keys, q_t[qi[s]])
        scores[w] = sc
        one = jnp.max(sc[0:HALF], axis=0, keepdims=True)
        two = jnp.max(sc[HALF : 2 * HALF], axis=0, keepdims=True)
        peak[w] = jnp.where(pairs[s] == 1, jnp.maximum(one, two), one) * SCALE

    def stage_weights(u, s, w, carry):
        m, l = carry
        new = first[s] == 1
        m = jnp.where(new, LOW if u == 0 else m_a[la[s]], m)
        l = jnp.where(new, 0.0 if u == 0 else l_a[la[s]], l)
        m_new = jnp.maximum(m, peak[w])
        m_two = jnp.where(pairs[s] == 1, m_new, -LOW)
        al = jnp.exp2(m - m_new)
        l = l * al
        for x, m_x in enumerate((m_new, m_two)):
            rows = pl.ds(x * HALF, HALF)
            p = jnp.exp2(scores[w, rows] * SCALE - m_x)
            l = l + jnp.sum(p, axis=0, keepdims=True)
            probs[w, rows] = p.astype(jnp.bfloat16)
        alpha[w] = al
        if u == 0:
            m_a[s] = m_new
            l_a[s] = l
        else:
            total[w] = l
        return m_new, l

    def stage_values(u, s, w):
        blocks = [kv[u][k[s], HALF + x * HD : HALF + (x + 1) * HD] for k in (k1, k2) for x in range(2)]
        d = dot_nn(jnp.concatenate(blocks, axis=1), probs[w])
        prev = acc[...]
        if u == 1:
            prev = jnp.where(first[s] == 1, slot_a[la[s]], prev)
        a = prev * alpha[w] + d
        acc[...] = a
        if u == 0:
            slot_a[s] = a
        else:
            slot_b[s] = (a * (1.0 / total[w])).T.astype(jnp.bfloat16)

    def attend(u, beside):
        ahead_s, ahead_w = 4, 2
        acc[...] = jnp.zeros_like(acc)
        carry = (jnp.zeros((1, HALF), jnp.float32), jnp.zeros((1, HALF), jnp.float32))
        for s in range(ahead_s):
            stage_scores(u, s, s)
        for s in range(ahead_w):
            carry = stage_weights(u, s, s, carry)

        def body(t, carry):
            for w in range(UNROLL):
                s = t * UNROLL + w
                stage_values(u, s, w)
                stage_scores(u, s + ahead_s, (w + ahead_s) % UNROLL)
                carry = stage_weights(u, s + ahead_w, (w + ahead_w) % UNROLL, carry)
            beside(t)
            return carry

        lax.fori_loop(0, UNITS // UNROLL, body, carry)

    def forwards_due(t):
        return jnp.clip(t - 2, 0, CHIPS - 1)

    def beside_a(t):
        lax.fori_loop(forwards_due(t), forwards_due(t + 1), forward(1), 0)

    attend(0, beside_a)
    lax.fori_loop(UNITS // UNROLL - 2, CHIPS - 1, forward(1), 0)
    own_kv[1].wait()
    kv_arrive(1)

    def o_copy(jj):
        out_rows = pl.ds(pl.multiple_of(core * HALF, HALF), HALF)
        return remote(o_send.at[jj], out_hbm.at[out_rows, cols(chip)], s_o.at[jj], r_o.at[me], target(me, jj))

    own_o = pltpu.make_async_copy(o_send.at[DEVS - 1], out_hbm.at[own_rows, cols(chip)], s_own.at[3])

    def emit(jj, _):
        o_send[jj] = slot_b[last[jj]]

        @pl.when(jj < DEVS - 1)
        def _():
            o_copy(jj).start()

        @pl.when(jj == DEVS - 1)
        def _():
            own_o.start()

        return 0

    def outputs_due(t):
        s = t * UNROLL
        return jnp.clip(jnp.maximum(s // MAX_UNITS, s - (MOST - DEVS)), 0, DEVS)

    def beside_b(t):
        lax.fori_loop(outputs_due(t), outputs_due(t + 1), emit, 0)

    attend(1, beside_b)

    def q_sent(jj, _):
        q_copy(jj).wait_send()
        return 0

    lax.fori_loop(0, DEVS - 1, q_sent, 0)
    for u in range(2):

        def kv_sent(n, _, u=u):
            kv_copy(u, n).wait_send()
            forward_copy(u, n).wait_send()
            return 0

        lax.fori_loop(0, CHIPS - 1, kv_sent, 0)
        own_fwd[u].wait_send()

    def o_sent(jj, _):
        o_copy(jj).wait_send()
        return 0

    lax.fori_loop(0, DEVS - 1, o_sent, 0)
    own_o.wait()

    def o_arrive(d, _):
        p = (me + d) % DEVS
        rows = pl.ds(pl.multiple_of((p % 2) * HALF, HALF), HALF)
        remote(o_send.at[0], out_hbm.at[rows, cols(p // 2)], s_o.at[0], r_o.at[p], partner).wait_recv()
        return 0

    lax.fori_loop(1, DEVS, o_arrive, 0)


def local(queries, keys_values, image_tiles, loader_tiles):
    bf16, f32 = jnp.bfloat16, jnp.float32
    anywhere = pl.BlockSpec(memory_space=pl.ANY)
    smem = pl.BlockSpec(memory_space=pltpu.SMEM)
    dma = pltpu.SemaphoreType.DMA

    vmem = pl.BlockSpec(memory_space=pltpu.VMEM)
    lists = pl.pallas_call(
        list_kernel,
        out_shape=jax.ShapeDtypeStruct((8, LISTS), jnp.int32),
        in_specs=[smem] * 2,
        out_specs=vmem,
        name="lists",
    )(image_tiles, loader_tiles)
    return pl.pallas_call(
        attend_kernel,
        out_shape=jax.ShapeDtypeStruct(queries.shape, bf16),
        in_specs=[anywhere] * 2 + [smem],
        out_specs=anywhere,
        scratch_shapes=[
            pltpu.VMEM((CHIPS, 2 * HALF, 2, HD), bf16),
            pltpu.VMEM((4 * HALF, HD), f32),
            pltpu.VMEM((CHIPS, 2, 2 * HALF, HD), bf16),
            pltpu.VMEM((DEVS, 2 * HALF, HD), bf16),
            pltpu.VMEM((DEVS, 2 * HALF, HD), bf16),
            pltpu.VMEM((DEVS, HALF, HD), bf16),
            pltpu.VMEM((DEVS, HD, HALF), bf16),
            pltpu.VMEM((UNROLL, 2 * HALF, HALF), f32),
            pltpu.VMEM((UNROLL, 2 * HALF, HALF), bf16),
            pltpu.VMEM((UNROLL, 1, HALF), f32),
            pltpu.VMEM((UNROLL, 1, HALF), f32),
            pltpu.VMEM((UNROLL, 1, HALF), f32),
            pltpu.VMEM((UNITS, HD, HALF), f32),
            pltpu.VMEM((LISTS, 1, HALF), f32),
            pltpu.VMEM((LISTS, 1, HALF), f32),
            pltpu.VMEM((HD, HALF), f32),
            pltpu.VMEM((UNITS, HALF, HD), bf16),
            pltpu.VMEM((DEVS, HALF, HD), bf16),
            dma((CHIPS,)),
            dma((DEVS,)),
            dma((DEVS,)),
            dma((2, CHIPS)),
            dma((2, DEVS)),
            dma((2, CHIPS)),
            dma((DEVS,)),
            dma((DEVS,)),
            dma((4,)),
        ],
        compiler_params=pltpu.CompilerParams(collective_id=0, has_side_effects=True, vmem_limit_bytes=51 << 20),
        name="attend",
    )(queries, keys_values, lists)


def solution(mesh):
    in_specs = (P(("dp", "seq"), None), P(("dp", "seq"), None, None), P("dp"), P("dp"))
    out_specs = P(("dp", "seq"), None)
    return jax.shard_map(local, mesh=mesh, in_specs=in_specs, out_specs=out_specs, check_vma=False)
```

```python
import functools

import jax
import jax.numpy as jnp
from jax import lax
from jax.experimental import pallas as pl
from jax.experimental.pallas import tpu as pltpu
from jax.sharding import PartitionSpec as P

MESH = pl.DeviceIdType.MESH
HD = 128
HALF = 256
SIDE = 4
CHIPS = 16
DEVS = 32
MAX_UNITS = 4
UNITS = 84
MOST = 83
UNROLL = 6
LISTS = 128
SCALE = HD**-0.5 * 1.4426950408889634
LOW = -1e30


ORDER = ((2, 0), (0, 2), (2, 1), (2, 3), (1, 2), (3, 2), (2, 2), (1, 0), (3, 0), (0, 1), (0, 3), (1, 1), (3, 3), (1, 3), (3, 1))


def offset(n, core):
    a, b = jnp.zeros_like(n), jnp.zeros_like(n)
    for k, (along_z, along_x) in enumerate(ORDER):
        a = jnp.where(n == k, along_z, a)
        b = jnp.where(n == k, along_x, b)
    return jnp.where(core == 0, a, (SIDE - b) % SIDE), jnp.where(core == 0, b, (SIDE - a) % SIDE)


def chip_at(chip, n, core, sign=1):
    dz, dx = offset(n, core)
    z, x = chip // SIDE, chip % SIDE
    return ((z + SIDE + sign * dz) % SIDE) * SIDE + (x + SIDE + sign * dx) % SIDE


def target(me, jj):
    core, chip = me % 2, me // 2
    n, e = jj // 2, jj % 2
    return chip_at(chip, n, core) * 2 + (core + 1 - e) % 2


def list_kernel(tiles_ref, loader_ref, lists_ref):
    me = lax.axis_index("seq")
    f32 = jnp.float32
    images = tiles_ref.shape[0]

    def grid(shape, axis):
        return lax.broadcasted_iota(jnp.int32, shape, axis)

    def pick(mask, values, axis):
        return jnp.sum(jnp.where(mask, values, 0.0), axis=axis, keepdims=True)

    def across(ref):
        n = ref.shape[0]
        values = jnp.zeros((1, n), jnp.int32)
        for i in range(n):
            values = jnp.where(grid((1, n), 1) == i, ref[i], values)
        return values.astype(f32)

    tiles, loader = across(tiles_ref), across(loader_ref)
    row, col = grid((DEVS, DEVS), 0), grid((DEVS, DEVS), 1)
    image_row, image_col = grid((images, images), 0), grid((images, images), 1)
    loader_down = pick(row == col, loader, 1)
    tiles_down = pick(image_row == image_col, tiles, 1)
    ends = pick(image_row <= image_col, tiles_down, 0)
    starts = ends - tiles
    place = target(me, grid((DEVS, 1), 0))
    tile = pick(place == col, loader, 1)
    lo, hi = pick(ends <= tile, tiles, 1), pick(starts <= tile, tiles, 1)
    count = jnp.floor((hi - lo + 1.0) * 0.5)
    after = pick(col <= row, pick(row == col, count, 0), 1)
    before = after - count
    s = grid((1, LISTS), 1).astype(f32)
    mine = (before <= s) & (s < after)
    r = s - pick(mine, before, 0)
    one = pick(mine, lo, 0) + 2.0 * r
    two = jnp.minimum(one + 1.0, pick(mine, hi, 0) - 1.0)
    down = grid((DEVS, LISTS), 0)
    devices = down.astype(f32)
    live = s < jnp.sum(count, axis=0, keepdims=True)
    lists = (
        pick(mine, place.astype(f32), 0),
        pick(loader_down == one, devices, 0),
        pick(loader_down == two, devices, 0),
        jnp.where(live, two - one, 0.0),
        jnp.where(live, jnp.where(r == 0.0, 1.0, 0.0), 1.0),
        pick(mine, after - 1.0, 0),
        pick(down == grid((DEVS, LISTS), 1), after - 1.0, 0),
    )
    for i, values in enumerate(lists):
        lists_ref[i : i + 1, :] = values.astype(jnp.int32)
    lists_ref[len(lists) : len(lists) + 1, :] = jnp.zeros((1, LISTS), jnp.int32)


def dot_nn(a, b):
    return lax.dot_general(a, b, (((1,), (0,)), ((), ())), preferred_element_type=jnp.float32)


def attend_kernel(
    q_hbm,
    kv_hbm,
    lists,
    out_hbm,
    pair,
    wide,
    stage,
    kv_a,
    kv_b,
    q,
    q_t,
    scores,
    probs,
    alpha,
    total,
    peak,
    slot_a,
    m_a,
    l_a,
    acc,
    slot_b,
    o_send,
    s_pair,
    s_q,
    r_q,
    s_kv,
    r_kv,
    s_fwd,
    s_o,
    r_o,
    s_own,
):
    me = lax.axis_index("seq")
    core, chip = me % 2, me // 2
    partner = chip * 2 + 1 - core
    kv = (kv_a, kv_b)
    qi, k1, k2, pairs, first, la, last = [lists.at[i] for i in range(7)]

    def remote(src, dst, send, recv, device):
        return pltpu.make_async_remote_copy(
            src_ref=src, dst_ref=dst, send_sem=send, recv_sem=recv, device_id={"seq": device}, device_id_type=MESH
        )

    def cols(head):
        return pl.ds(pl.multiple_of(head * HD, HD), HD)

    def pair_load(head):
        return pltpu.make_async_copy(kv_hbm.at[:, :, cols(head)], pair.at[head], s_pair.at[head])

    def pair_loads(n, _):
        pair_load(chip_at(chip, n, core)).start()
        return 0

    lax.fori_loop(0, CHIPS, pair_loads, 0)

    barrier = pltpu.get_barrier_semaphore()
    for d in range(1, DEVS):
        pl.semaphore_signal(barrier, inc=1, device_id={"seq": (me + d) % DEVS}, device_id_type=MESH)
    pl.semaphore_wait(barrier, DEVS - 1)

    def q_copy(jj):
        device = target(me, jj)
        rows = pl.ds(pl.multiple_of((device % 2) * HALF, HALF), HALF)
        return remote(q_hbm.at[rows, cols(device // 2)], q.at[me], s_q.at[jj], r_q.at[me], device)

    def q_sends(jj, _):
        q_copy(jj).start()
        return 0

    lax.fori_loop(0, DEVS - 1, q_sends, 0)
    own_rows = pl.ds(pl.multiple_of(core * HALF, HALF), HALF)
    own_q = pltpu.make_async_copy(q_hbm.at[own_rows, cols(chip)], q.at[me], s_own.at[0])
    own_q.start()

    def kv_copy(u, n):
        t = chip_at(chip, n, core)
        return remote(stage.at[t, u], kv[u].at[me], s_kv.at[u, n], r_kv.at[u, me], t * 2 + core)

    def split(n, _):
        t = chip_at(chip, n, core)
        pair_load(t).wait()
        wide[...] = pair[t].reshape(2 * 2 * HALF, HD).astype(jnp.float32)
        keys = wide[pl.ds(0, 2 * HALF, stride=2), :].astype(jnp.bfloat16)
        values = wide[pl.ds(1, 2 * HALF, stride=2), :].T.astype(jnp.bfloat16)
        for u in range(2):
            stage[t, u, 0:HALF] = keys[u * HALF : (u + 1) * HALF]
            stage[t, u, HALF : HALF + HD] = values[:, u * HALF : u * HALF + HD]
            stage[t, u, HALF + HD : 2 * HALF] = values[:, u * HALF + HD : (u + 1) * HALF]

        @pl.when(n < CHIPS - 1)
        def _():
            kv_copy(0, n).start()

        return 0

    lax.fori_loop(0, CHIPS, split, 0)

    def kv_sends(n, _):
        kv_copy(1, n).start()
        return 0

    lax.fori_loop(0, CHIPS - 1, kv_sends, 0)
    own_kv = [pltpu.make_async_copy(stage.at[chip, u], kv[u].at[me], s_own.at[1 + u]) for u in range(2)]
    own_fwd = [
        remote(stage.at[chip, u], kv[u].at[me], s_fwd.at[u, CHIPS - 1], r_kv.at[u, me], partner) for u in range(2)
    ]
    for u in range(2):
        own_kv[u].start()
        own_fwd[u].start()

    def forward_copy(u, n):
        p = chip_at(chip, n, core, -1) * 2 + core
        return remote(kv[u].at[p], kv[u].at[p], s_fwd.at[u, n], r_kv.at[u, p], partner)

    def forward(u):
        def step(n, _):
            copy = forward_copy(u, n)
            copy.wait_recv()
            copy.start()
            return 0

        return step

    def kv_arrive(u):
        def step(c, _):
            p = c * 2 + 1 - core
            remote(kv[u].at[p], kv[u].at[p], s_fwd.at[u, 0], r_kv.at[u, p], partner).wait_recv()
            return 0

        lax.fori_loop(0, CHIPS, step, 0)

    def q_arrive(d, _):
        p = (me + d) % DEVS
        remote(q.at[p], q.at[p], s_q.at[0], r_q.at[p], partner).wait_recv()
        return 0

    lax.fori_loop(1, DEVS, q_arrive, 0)
    own_q.wait()

    def turn(p, _):
        q_t[p] = q[p].T
        return 0

    lax.fori_loop(0, DEVS, turn, 0)
    lax.fori_loop(0, CHIPS - 1, forward(0), 0)
    own_kv[0].wait()
    kv_arrive(0)

    def stage_scores(u, s, w):
        keys = jnp.concatenate([kv[u][k1[s], 0:HALF], kv[u][k2[s], 0:HALF]], axis=0)
        sc = dot_nn(keys, q_t[qi[s]])
        scores[w] = sc
        one = jnp.max(sc[0:HALF], axis=0, keepdims=True)
        two = jnp.max(sc[HALF : 2 * HALF], axis=0, keepdims=True)
        peak[w] = jnp.where(pairs[s] == 1, jnp.maximum(one, two), one) * SCALE

    def stage_weights(u, s, w, carry):
        m, l = carry
        new = first[s] == 1
        m = jnp.where(new, LOW if u == 0 else m_a[la[s]], m)
        l = jnp.where(new, 0.0 if u == 0 else l_a[la[s]], l)
        m_new = jnp.maximum(m, peak[w])
        m_two = jnp.where(pairs[s] == 1, m_new, -LOW)
        al = jnp.exp2(m - m_new)
        l = l * al
        for x, m_x in enumerate((m_new, m_two)):
            rows = pl.ds(x * HALF, HALF)
            p = jnp.exp2(scores[w, rows] * SCALE - m_x)
            l = l + jnp.sum(p, axis=0, keepdims=True)
            probs[w, rows] = p.astype(jnp.bfloat16)
        alpha[w] = al
        if u == 0:
            m_a[s] = m_new
            l_a[s] = l
        else:
            total[w] = l
        return m_new, l

    def stage_values(u, s, w):
        blocks = [kv[u][k[s], HALF + x * HD : HALF + (x + 1) * HD] for k in (k1, k2) for x in range(2)]
        d = dot_nn(jnp.concatenate(blocks, axis=1), probs[w])
        prev = acc[...]
        if u == 1:
            prev = jnp.where(first[s] == 1, slot_a[la[s]], prev)
        a = prev * alpha[w] + d
        acc[...] = a
        if u == 0:
            slot_a[s] = a
        else:
            slot_b[s] = (a * (1.0 / total[w])).T.astype(jnp.bfloat16)

    def attend(u, beside):
        ahead_s, ahead_w = 4, 2
        acc[...] = jnp.zeros_like(acc)
        carry = (jnp.zeros((1, HALF), jnp.float32), jnp.zeros((1, HALF), jnp.float32))
        for s in range(ahead_s):
            stage_scores(u, s, s)
        for s in range(ahead_w):
            carry = stage_weights(u, s, s, carry)

        def body(t, carry):
            for w in range(UNROLL):
                s = t * UNROLL + w
                stage_values(u, s, w)
                stage_scores(u, s + ahead_s, (w + ahead_s) % UNROLL)
                carry = stage_weights(u, s + ahead_w, (w + ahead_w) % UNROLL, carry)
            beside(t)
            return carry

        lax.fori_loop(0, UNITS // UNROLL, body, carry)

    def forwards_due(t):
        return jnp.clip(t - 2, 0, CHIPS - 1)

    def beside_a(t):
        lax.fori_loop(forwards_due(t), forwards_due(t + 1), forward(1), 0)

    attend(0, beside_a)
    lax.fori_loop(UNITS // UNROLL - 2, CHIPS - 1, forward(1), 0)
    own_kv[1].wait()
    kv_arrive(1)

    def o_copy(jj):
        out_rows = pl.ds(pl.multiple_of(core * HALF, HALF), HALF)
        return remote(o_send.at[jj], out_hbm.at[out_rows, cols(chip)], s_o.at[jj], r_o.at[me], target(me, jj))

    own_o = pltpu.make_async_copy(o_send.at[DEVS - 1], out_hbm.at[own_rows, cols(chip)], s_own.at[3])

    def emit(jj, _):
        o_send[jj] = slot_b[last[jj]]

        @pl.when(jj < DEVS - 1)
        def _():
            o_copy(jj).start()

        @pl.when(jj == DEVS - 1)
        def _():
            own_o.start()

        return 0

    def outputs_due(t):
        s = t * UNROLL
        return jnp.clip(jnp.maximum(s // MAX_UNITS, s - (MOST - DEVS)), 0, DEVS)

    def beside_b(t):
        lax.fori_loop(outputs_due(t), outputs_due(t + 1), emit, 0)

    attend(1, beside_b)

    def q_sent(jj, _):
        q_copy(jj).wait_send()
        return 0

    lax.fori_loop(0, DEVS - 1, q_sent, 0)
    for u in range(2):

        def kv_sent(n, _, u=u):
            kv_copy(u, n).wait_send()
            forward_copy(u, n).wait_send()
            return 0

        lax.fori_loop(0, CHIPS - 1, kv_sent, 0)
        own_fwd[u].wait_send()

    def o_sent(jj, _):
        o_copy(jj).wait_send()
        return 0

    lax.fori_loop(0, DEVS - 1, o_sent, 0)
    own_o.wait()

    def o_arrive(d, _):
        p = (me + d) % DEVS
        rows = pl.ds(pl.multiple_of((p % 2) * HALF, HALF), HALF)
        remote(o_send.at[0], out_hbm.at[rows, cols(p // 2)], s_o.at[0], r_o.at[p], partner).wait_recv()
        return 0

    lax.fori_loop(1, DEVS, o_arrive, 0)


def local(queries, keys_values, image_tiles, loader_tiles):
    bf16, f32 = jnp.bfloat16, jnp.float32
    anywhere = pl.BlockSpec(memory_space=pl.ANY)
    smem = pl.BlockSpec(memory_space=pltpu.SMEM)
    dma = pltpu.SemaphoreType.DMA

    vmem = pl.BlockSpec(memory_space=pltpu.VMEM)
    lists = pl.pallas_call(
        list_kernel,
        out_shape=jax.ShapeDtypeStruct((8, LISTS), jnp.int32),
        in_specs=[smem] * 2,
        out_specs=vmem,
        name="lists",
    )(image_tiles, loader_tiles)
    return pl.pallas_call(
        attend_kernel,
        out_shape=jax.ShapeDtypeStruct(queries.shape, bf16),
        in_specs=[anywhere] * 2 + [smem],
        out_specs=anywhere,
        scratch_shapes=[
            pltpu.VMEM((CHIPS, 2 * HALF, 2, HD), bf16),
            pltpu.VMEM((4 * HALF, HD), f32),
            pltpu.VMEM((CHIPS, 2, 2 * HALF, HD), bf16),
            pltpu.VMEM((DEVS, 2 * HALF, HD), bf16),
            pltpu.VMEM((DEVS, 2 * HALF, HD), bf16),
            pltpu.VMEM((DEVS, HALF, HD), bf16),
            pltpu.VMEM((DEVS, HD, HALF), bf16),
            pltpu.VMEM((UNROLL, 2 * HALF, HALF), f32),
            pltpu.VMEM((UNROLL, 2 * HALF, HALF), bf16),
            pltpu.VMEM((UNROLL, 1, HALF), f32),
            pltpu.VMEM((UNROLL, 1, HALF), f32),
            pltpu.VMEM((UNROLL, 1, HALF), f32),
            pltpu.VMEM((UNITS, HD, HALF), f32),
            pltpu.VMEM((LISTS, 1, HALF), f32),
            pltpu.VMEM((LISTS, 1, HALF), f32),
            pltpu.VMEM((HD, HALF), f32),
            pltpu.VMEM((UNITS, HALF, HD), bf16),
            pltpu.VMEM((DEVS, HALF, HD), bf16),
            dma((CHIPS,)),
            dma((DEVS,)),
            dma((DEVS,)),
            dma((2, CHIPS)),
            dma((2, DEVS)),
            dma((2, CHIPS)),
            dma((DEVS,)),
            dma((DEVS,)),
            dma((4,)),
        ],
        compiler_params=pltpu.CompilerParams(collective_id=0, has_side_effects=True, vmem_limit_bytes=51 << 20),
        name="attend",
    )(queries, keys_values, lists)


def solution(mesh):
    in_specs = (P(("dp", "seq"), None), P(("dp", "seq"), None, None), P("dp"), P("dp"))
    out_specs = P(("dp", "seq"), None)
    return jax.shard_map(local, mesh=mesh, in_specs=in_specs, out_specs=out_specs, check_vma=False)
```
